256 devices in a mesh: leaf: 64 (over y, z, core), rhs: 4 (over x).
Axes of the slice: x: 4, y: 4, z: 8, core: 2. Of those that a mesh axis runs over, the one named last changes fastest.
Arguments:
- leaf_right: float32 [2048, 256, 128], P('leaf', 'rhs'), may hold values from -6 to 6
- upper_right: float32 [128, 256, 128], P('leaf', 'rhs'), may hold values from -6 to 6
- leaf_inverse: bfloat16 [2048, 128, 128], P(('leaf', 'rhs')), as said below
- upper_inverse: bfloat16 [128, 128, 128], P('leaf'), as said below
- update_blocks: bfloat16 [16384, 128, 128], P('leaf'), may hold values from -0.046875 to 0.046875
- block_target: int32 [16384, 1], P('leaf'), may hold values from 0 to 127; in each aligned block of 256 rows (0 to 255, 256 to 511, ...) at most 4 rows name the same one
- upper_place: int32 [128], replicated, may hold values from 0 to 127, each once
Outputs:
- leaf_solution: float32 [2048, 256, 128], P('leaf', 'rhs')
- upper_solution: float32 [128, 256, 128], P('leaf', 'rhs')
The draws below stay inside these ranges and needn't reach their ends.
Inputs may be any that keep to these rules, and one draw needn't show every extreme that they name: `leaf_inverse`: lower triangular blocks, diagonal entries between 0.6 and 1.4. `upper_inverse`: lower triangular blocks, diagonal entries between 0.6 and 1.4. `block_target`: among the 256 blocks of one device no upper supernode is named more than 4 times, a bound that some block reaches. `upper_place`: each row of the upper arrays holds exactly one upper supernode.
All inputs are finite; a program needn't handle non-finite values.
Results may differ from the reference program's by a relative error of at most 0.0049.
Values may be sent and summed in bfloat16 or wider, within the bound.
A program may use at most 64 MiB of HBM per device.

```python
import math
import jax
import jax.numpy as jnp
import numpy as np
from jax import lax

W = 128
RHS = 256
B = 8
S0 = 32
S1 = 2
N0 = 2048
NS1 = 128
CAP = 4
N_LEAF = 64


def triangle_blocks(key, number):
    lower_key, diagonal_key = jax.random.split(key)
    lower = jax.random.normal(lower_key, (number, W, W), jnp.float32)
    lower = lower * (0.8 * W ** (-0.5))
    diagonal = jax.random.uniform(diagonal_key, (number, W), jnp.float32, 0.6, 1.4)
    row_index = jnp.arange(W)[:, None]
    column_index = jnp.arange(W)[None, :]
    below = row_index > column_index
    on_diagonal = row_index == column_index
    block = jnp.where(below[None], lower, 0.0) + jnp.where(on_diagonal[None], diagonal[:, :, None], 0.0)
    return block.astype(jnp.bfloat16)


def draw_leaf_inverse(key, part):
    return triangle_blocks(jax.random.fold_in(key, 11), N0)


def draw_upper_inverse(key, part):
    return triangle_blocks(jax.random.fold_in(key, 23), NS1)


def steps_of(stream_key, dims, cuts, smallest, high):
    factor_of = 1.0
    for dim, parts in cuts:
        heights = jax.random.uniform(jax.random.fold_in(jax.random.fold_in(stream_key, 6), dim), (parts,), jnp.float32, smallest / len(cuts), high / len(cuts))
        factor_of = factor_of * jnp.repeat(jnp.exp(heights), dims[dim] // parts).reshape((-1,) + (1,) * (len(dims) - 1 - dim))
    return factor_of


def assign_block(stream_key, own, number, rows, count, top, most, skew):
    order = jax.random.permutation(stream_key, count)
    packed, ordinary = portions_of(count, rows * top, most, skew, True), portions_of(count, rows * top, most, skew, False)
    places = jnp.arange(count)

    def named(lengths, offset_by):
        used = int((lengths > 0).sum())
        fixed = max(1, used // 4)
        passed = fixed + (places - fixed + offset_by * (used - fixed)) % max(1, count - fixed)
        return jnp.zeros((count,), jnp.int32).at[order[jnp.where(places < fixed, places, passed)]].set(jnp.asarray(lengths, jnp.int32))

    lengths = jnp.where(number % 4 == 0, named(packed, number // 4), named(ordinary, number - number // 4 - 1))
    mixed = jax.random.permutation(jax.random.fold_in(own, 3), count)
    source_of, sink = mixed[0:count // 2 * 2:2], mixed[1:count // 2 * 2:2]
    margin = jnp.minimum(lengths[source_of] - 1, most - lengths[sink]) // 2
    margin = jnp.where((source_of == order[0]) | (sink == order[0]) | (lengths[sink] == 0), 0, jnp.maximum(margin, 0))
    passed = jax.random.randint(jax.random.fold_in(own, 4), (count // 2,), 0, 1 << 20) % (margin + 1)
    lengths = lengths.at[source_of].add(-passed).at[sink].add(passed)
    items = jnp.searchsorted(jnp.cumsum(lengths), jnp.arange(rows * top), side="right").astype(jnp.int32)
    listing = items.reshape(top, rows).T
    listing = listing[jax.random.permutation(jax.random.fold_in(own, 1), rows)]
    offset_by = jax.random.randint(jax.random.fold_in(own, 2), (rows, 1), 0, top)
    return jnp.take_along_axis(listing, (jnp.arange(top)[None, :] + offset_by) % top, axis=1)


def portions_of(number_of, total, reach, slope, full):
    loads = [(1 << 20) // math.isqrt(rank ** slope) + 1 for rank in range(1, number_of + 1)]
    largest = reach if full else min(reach, max(-(-total // number_of), total * loads[0] // sum(loads)))
    least = 1 if total - largest >= number_of - 1 else 0
    holding, rest = [largest] + [least] * (number_of - 1), total - largest - least * (number_of - 1)
    while rest > 0:
        movable = [i for i in range(1, number_of) if holding[i] < largest] or [i for i in range(1, number_of) if holding[i] < reach]
        pool, budget = sum([loads[i] for i in movable]), rest
        for i in movable:
            more = min(reach - holding[i], max(1, budget * loads[i] // pool), rest)
            holding[i] = holding[i] + more
            rest = rest - more
    return np.array(holding)


def gaussian(rng, shape, spread, bound, cuts=(), kind=jnp.bfloat16):
    array = spread * jax.random.normal(rng, shape, jnp.float32)
    if cuts:
        array = array * steps_of(rng, shape, cuts, -0.22, 0.18)
    return jnp.clip(array, -bound, bound).astype(kind)


def setup_inputs(seed: int = 0) -> dict:
    key_of = jax.random.split(jax.random.key(seed), 8)
    leaf_right = gaussian(key_of[0], (N0, RHS, W), 1.0, 6.0, ((0, 64), (1, 4)), jnp.float32)
    upper_right = gaussian(key_of[1], (NS1, RHS, W), 1.0, 6.0, ((0, 64), (1, 4)), jnp.float32)
    leaf_inverse = draw_leaf_inverse(jax.random.fold_in(key_of[7], 71), 0)
    upper_inverse = draw_upper_inverse(jax.random.fold_in(key_of[7], 71), 0)
    update_blocks = gaussian(key_of[4], (N0 * B, W, W), (W * S0 * B // S1) ** -0.5, 0.046875, ((0, 64),))
    block_target_keys = jax.random.split(jax.random.fold_in(key_of[5], 1), (N0 * B) // (S0 * B))
    block_target_turns = jax.random.permutation(jax.random.fold_in(key_of[5], 3), (N0 * B) // (S0 * B))
    block_target = jax.vmap(lambda own, number: assign_block(jax.random.fold_in(key_of[5], 2), own, number, S0 * B, NS1, 1, CAP, 2))(block_target_keys, block_target_turns).reshape((N0 * B, 1))
    upper_place = jax.random.permutation(key_of[6], NS1).astype(jnp.int32)
    return {"leaf_right": leaf_right, "upper_right": upper_right, "leaf_inverse": leaf_inverse, "upper_inverse": upper_inverse, "update_blocks": update_blocks, "block_target": block_target, "upper_place": upper_place}


def to_half(values):
    return lax.optimization_barrier(values.astype(jnp.bfloat16)).astype(jnp.float32)


def reference(leaf_right, upper_right, leaf_inverse, upper_inverse, update_blocks, block_target, upper_place):
    inverse_wide = leaf_inverse.astype(jnp.float32)
    leaf_rounded = to_half(leaf_right)
    leaf_forward = jnp.einsum('ncw,nvw->ncv', leaf_rounded, inverse_wide)
    leaf_half = to_half(leaf_forward)
    position = upper_place[block_target[:, 0]].astype(jnp.int32)
    span_ids = jnp.arange(N_LEAF, dtype=jnp.int32)

    def forward_span(total, index):
        solved = lax.dynamic_slice_in_dim(leaf_half, index * S0, S0, 0)
        blocks = lax.dynamic_slice_in_dim(update_blocks, index * S0 * B, S0 * B, 0).astype(jnp.float32)
        blocks = blocks.reshape(S0, B, W, W)
        where_to = lax.dynamic_slice_in_dim(position, index * S0 * B, S0 * B, 0)
        terms = jnp.einsum('ncw,nbvw->nbcv', solved, blocks).reshape(S0 * B, RHS, W)
        return total + jax.ops.segment_sum(terms, where_to, num_segments=NS1), None

    upper_sums, unused = lax.scan(forward_span, jnp.zeros((NS1, RHS, W), jnp.float32), span_ids)
    upper_rounded = to_half(upper_right - upper_sums)
    upper_wide = upper_inverse.astype(jnp.float32)
    upper_half = to_half(jnp.einsum('pcw,pvw->pcv', upper_rounded, upper_wide))
    upper_solution = jnp.einsum('pcw,pwv->pcv', upper_half, upper_wide)
    upper_sent = to_half(upper_solution)

    def backward_span(index):
        where_to = lax.dynamic_slice_in_dim(position, index * S0 * B, S0 * B, 0)
        chosen = upper_sent[where_to]
        blocks = lax.dynamic_slice_in_dim(update_blocks, index * S0 * B, S0 * B, 0).astype(jnp.float32)
        corrections = jnp.einsum('kcv,kvw->kcw', chosen, blocks).reshape(S0, B, RHS, W).sum(axis=1)
        solved = lax.dynamic_slice_in_dim(leaf_forward, index * S0, S0, 0)
        leaf_back = to_half(solved - corrections)
        inverse_part = lax.dynamic_slice_in_dim(inverse_wide, index * S0, S0, 0)
        return jnp.einsum('ncw,nwv->ncv', leaf_back, inverse_part)

    leaf_solution = lax.map(backward_span, span_ids).reshape(N0, RHS, W)
    return leaf_solution, upper_solution
```

```python
import functools

import jax
import jax.numpy as jnp
from jax import lax
from jax.experimental import pallas as pl
from jax.experimental.pallas import tpu as pltpu
from jax.sharding import PartitionSpec as P

MESH = pl.DeviceIdType.MESH
F32, BF16, I32 = jnp.float32, jnp.bfloat16, jnp.int32
NX, NY, NZ, NC = 4, 4, 8, 2
PER = 8
GROUP = 8
COLS, W = 64, 128
BLOCKS = 256
CAP = 4
UPPER = NY * NZ * NC * 2
NT = (((1,), (1,)), ((), ()))
NN = (((1,), (0,)), ((), ()))


def kernel(
    target_ref, place_ref, right_hbm, upper_right_hbm, inv_hbm, upper_inv_hbm, u_hbm,
    leaf_out, upper_out,
    u, x, inv, lf, t, idx_v, idx_s, a0, r0, o1, r1, o2, r2, ur, ui, us, g, lo,
    loc, xs, xr, cs, cr, ys, yr, zs, zr, azs, azr, ays, ayr, acs, acr,
):
    leaf, rx = lax.axis_index("leaf"), lax.axis_index("rhs")
    y, z, c = leaf // (NZ * NC), (leaf // NC) % NZ, leaf % NC

    def at(yy, zz, cc, xx):
        return ((yy * NZ + zz) * NC + cc, xx)

    def off_x(d):
        return at(y, z, c, (rx + d) % NX)

    def off_y(d):
        return at((y + d) % NY, z, c, rx)

    def off_z(d):
        return at(y, (z + d) % NZ, c, rx)

    sibling = at(y, z, 1 - c, rx)

    def remote(src, dst, ssem, rsem, dev):
        return pltpu.make_async_remote_copy(
            src_ref=src, dst_ref=dst, send_sem=ssem, recv_sem=rsem, device_id=dev, device_id_type=MESH
        )

    own = pltpu.make_async_copy(inv_hbm, inv.at[rx], loc.at[0])
    own.start()
    load_x = pltpu.make_async_copy(right_hbm, x, loc.at[1])
    load_x.start()
    order = (0, 1, 3, 2)
    load_u = []
    for i, d in enumerate(order):
        base = ((rx + NX - d) % NX) * (GROUP * PER)
        load_u.append(pltpu.make_async_copy(u_hbm.at[pl.ds(base, GROUP * PER)], u.at[pl.ds(base, GROUP * PER)], loc.at[2 + i]))
        load_u[-1].start()
    load_ur = pltpu.make_async_copy(upper_right_hbm, ur, loc.at[6])
    load_ur.start()
    load_ui = pltpu.make_async_copy(upper_inv_hbm, ui, loc.at[7])
    load_ui.start()

    barrier = pltpu.get_barrier_semaphore()
    peers = [off_x(d) for d in range(1, NX)] + [off_y(d) for d in range(1, NY)] + [off_z(d) for d in range(1, NZ)] + [sibling]
    for dev in peers:
        pl.semaphore_signal(barrier, inc=1, device_id=dev, device_id_type=MESH)

    lane = lax.broadcasted_iota(I32, (BLOCKS, W), 1)
    row = lax.broadcasted_iota(I32, (BLOCKS, W), 0)
    pos = jnp.sum(jnp.where(target_ref[...] == lane, place_ref[...], 0), axis=1, keepdims=True)
    cand = jnp.where(pos == lane, row, BLOCKS)
    for s in range(CAP):
        low = jnp.min(cand, axis=0, keepdims=True)
        idx_v[s : s + 1, :] = low
        cand = jnp.where(cand > low, cand, BLOCKS)
    where_in_g = ((pos // 2) % 2) * (UPPER // 2) + (pos // 4) * 2 + pos % 2
    for h in range(BLOCKS // W):
        idx_v[CAP + h : CAP + h + 1, :] = jnp.sum(jnp.where(row - h * W == lane, where_in_g, 0), axis=0, keepdims=True)
    idx_v[CAP + 2 :, :] = jnp.zeros((8 - CAP - 2, W), I32)
    to_smem = pltpu.make_async_copy(idx_v, idx_s, loc.at[8])
    to_smem.start()

    pl.semaphore_wait(barrier, len(peers))

    send_x = [remote(inv_hbm, inv.at[rx], xs.at[d - 1], xr.at[d - 1], off_x(d)) for d in (1, 3, 2)]
    for cp in send_x:
        cp.start()
    t[BLOCKS] = jnp.zeros((COLS, W), BF16)
    own.wait()
    load_x.wait()

    def forward(n, _):
        f = lax.dot_general(x[n].astype(BF16), inv[n // GROUP, n % GROUP], NT, preferred_element_type=F32)
        lf[n] = f
        r = lax.dot_general(f.astype(BF16), u[pl.ds(n * PER, PER)].reshape(PER * W, W), NT, preferred_element_type=F32)
        for b in range(PER):
            t[n * PER + b] = r[:, b * W : (b + 1) * W].astype(BF16)
        return 0

    for i, d in enumerate(order):
        src = (rx + NX - d) % NX
        if d:
            remote(inv_hbm, inv.at[src], xs.at[d - 1], xr.at[d - 1], off_x(d)).wait_recv()
        load_u[i].wait()
        lax.fori_loop(src * GROUP, src * GROUP + GROUP, forward, 0)
    to_smem.wait()

    def sum_of(p):
        total = t[idx_s[0, p]].astype(F32)
        for s in range(1, CAP):
            total = total + t[idx_s[s, p]].astype(F32)
        return total

    y_order = (2, 1, 3, 0)

    def place(d, zz, cc, j):
        return ((((y + d) % NY) * NZ + zz) * NC + cc) * 2 + j

    send_c = []
    for j in range(2):
        for d in y_order:
            def to_sibling(zz, _, d=d, j=j):
                a0[j, d, zz] = sum_of(place(d, zz, 1 - c, j)).astype(BF16)
                return 0

            lax.fori_loop(0, NZ, to_sibling, 0)
            cp = remote(a0.at[j, d], r0.at[j, d], cs.at[j, d], cr.at[j, d], sibling)
            cp.start()
            send_c.append(cp)
    send_y = []
    for j in range(2):
        for d in y_order:
            remote(a0.at[j, d], r0.at[j, d], cs.at[j, d], cr.at[j, d], sibling).wait_recv()

            def to_y(zz, _, d=d, j=j):
                o1[j, d, zz] = (sum_of(place(d, zz, c, j)) + r0[j, d, zz].astype(F32)).astype(BF16)
                return 0

            lax.fori_loop(0, NZ, to_y, 0)
            if d:
                cp = remote(o1.at[j, d], r1.at[j, d], ys.at[j, d], yr.at[j, d], off_y(d))
                cp.start()
                send_y.append(cp)
    send_z = []
    for j in range(2):
        for d in (2, 1, 3):
            remote(o1.at[j, d], r1.at[j, d], ys.at[j, d], yr.at[j, d], off_y(d)).wait_recv()
        for dz in (4, 3, 5, 2, 6, 1, 7, 0):
            zz = (z + dz) % NZ
            total = o1[j, 0, zz].astype(F32)
            for d in range(1, NY):
                total = total + r1[j, d, zz].astype(F32)
            o2[j, dz] = total.astype(BF16)
            if dz:
                cp = remote(o2.at[j, dz], r2.at[j, dz], zs.at[j, dz], zr.at[j, dz], off_z(dz))
                cp.start()
                send_z.append(cp)
    load_ur.wait()
    load_ui.wait()
    send_az = []
    mine = (y * NZ + z) * 2
    for j in range(2):
        total = o2[j, 0].astype(F32)
        for dz in range(1, NZ):
            remote(o2.at[j, dz], r2.at[j, dz], zs.at[j, dz], zr.at[j, dz], off_z(dz)).wait_recv()
            total = total + r2[j, dz].astype(F32)
        v = (ur[j] - total).astype(BF16)
        h = lax.dot_general(v, ui[j], NT, preferred_element_type=F32).astype(BF16)
        s = lax.dot_general(h, ui[j], NN, preferred_element_type=F32)
        us[j] = s
        g[c, mine + j] = s.astype(BF16)
    store_us = pltpu.make_async_copy(us, upper_out, loc.at[9])
    store_us.start()
    blk = g.at[c, pl.ds(mine, 2)]
    for dz in (4, 3, 5, 2, 6, 1, 7):
        cp = remote(blk, blk, azs.at[dz], azr.at[dz], off_z(dz))
        cp.start()
        send_az.append(cp)
    send_ay = []
    for dz in (0, 1, 7, 2, 6, 3, 5, 4):
        b = g.at[c, pl.ds((y * NZ + (z + NZ - dz) % NZ) * 2, 2)]
        if dz:
            remote(b, b, azs.at[dz], azr.at[dz], off_z(dz)).wait_recv()
        for d in (2, 1, 3):
            cp = remote(b, b, ays.at[d, dz], ayr.at[d, dz], off_y(d))
            cp.start()
            send_ay.append(cp)
        cp = remote(b, b, acs.at[0, dz], acr.at[0, dz], sibling)
        cp.start()
        send_ay.append(cp)
    for dz in (0, 1, 7, 2, 6, 3, 5, 4):
        for d in (1, 3, 2):
            b = g.at[c, pl.ds((((y + NY - d) % NY) * NZ + (z + NZ - dz) % NZ) * 2, 2)]
            remote(b, b, ays.at[d, dz], ayr.at[d, dz], off_y(d)).wait_recv()
            cp = remote(b, b, acs.at[d, dz], acr.at[d, dz], sibling)
            cp.start()
            send_ay.append(cp)
    for dz in (0, 1, 7, 2, 6, 3, 5, 4):
        for d in range(NY):
            b = g.at[1 - c, pl.ds((((y + NY - d) % NY) * NZ + (z + NZ - dz) % NZ) * 2, 2)]
            remote(b, b, acs.at[d, dz], acr.at[d, dz], sibling).wait_recv()

    def backward(n, _):
        parts = []
        for b in range(PER):
            k = n * PER + b
            e = idx_s[CAP + k // W, k % W]
            parts.append(g[e // (UPPER // 2), e % (UPPER // 2)])
        corr = lax.dot_general(
            jnp.concatenate(parts, axis=1), u[pl.ds(n * PER, PER)].reshape(PER * W, W), NN, preferred_element_type=F32
        )
        back = (lf[n] - corr).astype(BF16)
        lo[n] = lax.dot_general(back, inv[n // GROUP, n % GROUP], NN, preferred_element_type=F32)
        return 0

    stores = []
    for i in range(4):
        lax.fori_loop(i * GROUP, (i + 1) * GROUP, backward, 0)
        part = pl.ds(i * GROUP, GROUP)
        cp = pltpu.make_async_copy(lo.at[part], leaf_out.at[part], loc.at[10 + i])
        cp.start()
        stores.append(cp)
    for cp in send_x + send_c + send_y + send_z + send_az + send_ay:
        cp.wait_send()
    store_us.wait()
    for cp in stores:
        cp.wait()


def on_device(leaf_right, upper_right, leaf_inverse, upper_inverse, update_blocks, block_target, upper_place):
    any_space = pl.BlockSpec(memory_space=pl.ANY)
    vmem = pl.BlockSpec(memory_space=pltpu.VMEM)
    dma = pltpu.SemaphoreType.DMA
    leaves = NX * GROUP
    return pl.pallas_call(
        kernel,
        out_shape=(
            jax.ShapeDtypeStruct((leaves, COLS, W), F32),
            jax.ShapeDtypeStruct((2, COLS, W), F32),
        ),
        in_specs=[vmem, vmem] + [any_space] * 5,
        out_specs=(any_space, any_space),
        scratch_shapes=[
            pltpu.VMEM((BLOCKS, W, W), BF16),
            pltpu.VMEM((leaves, COLS, W), F32),
            pltpu.VMEM((NX, GROUP, W, W), BF16),
            pltpu.VMEM((leaves, COLS, W), F32),
            pltpu.VMEM((BLOCKS + 1, COLS, W), BF16),
            pltpu.VMEM((8, W), I32),
            pltpu.SMEM((8, W), I32),
            pltpu.VMEM((2, NY, NZ, COLS, W), BF16),
            pltpu.VMEM((2, NY, NZ, COLS, W), BF16),
            pltpu.VMEM((2, NY, NZ, COLS, W), BF16),
            pltpu.VMEM((2, NY, NZ, COLS, W), BF16),
            pltpu.VMEM((2, NZ, COLS, W), BF16),
            pltpu.VMEM((2, NZ, COLS, W), BF16),
            pltpu.VMEM((2, COLS, W), F32),
            pltpu.VMEM((2, W, W), BF16),
            pltpu.VMEM((2, COLS, W), F32),
            pltpu.VMEM((2, UPPER // 2, COLS, W), BF16),
            pltpu.VMEM((leaves, COLS, W), F32),
            dma((14,)),
            dma((3,)), dma((3,)),
            dma((2, NY)), dma((2, NY)),
            dma((2, NY)), dma((2, NY)),
            dma((2, NZ)), dma((2, NZ)),
            dma((NZ,)), dma((NZ,)),
            dma((NY, NZ)), dma((NY, NZ)),
            dma((NY, NZ)), dma((NY, NZ)),
        ],
        compiler_params=pltpu.CompilerParams(
            collective_id=0, has_side_effects=True, vmem_limit_bytes=56 * 2**20
        ),
        name="solve",
    )(block_target, upper_place.reshape(1, -1), leaf_right, upper_right, leaf_inverse, upper_inverse, update_blocks)


def solution(mesh):
    return jax.shard_map(
        on_device,
        mesh=mesh,
        in_specs=(
            P("leaf", "rhs", None),
            P("leaf", "rhs", None),
            P(("leaf", "rhs"), None, None),
            P("leaf", None, None),
            P("leaf", None, None),
            P("leaf", None),
            P(),
        ),
        out_specs=(P("leaf", "rhs", None), P("leaf", "rhs", None)),
        check_vma=False,
    )
```

```python
import jax
import jax.numpy as jnp
from jax import lax
from jax.experimental import pallas as pl
from jax.experimental.pallas import tpu as pltpu
from jax.sharding import PartitionSpec as P

MESH = pl.DeviceIdType.MESH
F32, BF16, I32 = jnp.float32, jnp.bfloat16, jnp.int32
NX, NY, NZ, NC = 4, 4, 8, 2
PER = 8
GROUP = 8
COLS, W = 64, 128
BLOCKS = 256
CAP = 4
UPPER = NY * NZ * NC * 2
STRIP = 16
NT = (((1,), (1,)), ((), ()))
NN = (((1,), (0,)), ((), ()))


def kernel(
    target_ref, place_ref, right_hbm, upper_right_hbm, inv_hbm, upper_inv_hbm, u_hbm,
    leaf_out, upper_out,
    u, x, pk, inv, lf, t, idx_v, idx_s, az, ay, bz, by, oz, oy, rzr, rzl, ryr, ryl,
    o2, r2, o3, r3, keep, ur, ui, us, g, lo,
    loc, xs, xr, csz, crz, csy, cry, zs, zr, ys, yr, s2, q2, s3, q3,
    azs, azr, ays, ayr, aws, awr, ars, arr, b1s, b1r, b0s, b0r,
):
    leaf, rx = lax.axis_index("leaf"), lax.axis_index("rhs")
    y, z, c = leaf // (NZ * NC), (leaf // NC) % NZ, leaf % NC

    def at(yy, zz, cc, xx):
        return ((yy * NZ + zz) * NC + cc, xx)

    def off_x(d):
        return at(y, z, c, (rx + d) % NX)

    def off_y(d):
        return at((y + d) % NY, z, c, rx)

    def off_z(d):
        return at(y, (z + d) % NZ, c, rx)

    sibling = at(y, z, 1 - c, rx)
    sends = []

    def remote(src, dst, ssem, rsem, dev):
        return pltpu.make_async_remote_copy(
            src_ref=src, dst_ref=dst, send_sem=ssem, recv_sem=rsem, device_id=dev, device_id_type=MESH
        )

    def send(src, dst, ssem, rsem, dev):
        cp = remote(src, dst, ssem, rsem, dev)
        cp.start()
        sends.append(cp)

    def arrived(ref, ssem, rsem, dev):
        remote(ref, ref, ssem, rsem, dev).wait_recv()

    own = pltpu.make_async_copy(inv_hbm, inv.at[rx], loc.at[0])
    own.start()

    def piece(i):
        d = jnp.where(i < 2, 0, jnp.where(i >= 6, 2, 1 + 2 * (i % 2)))
        half = jnp.where((i == 4) | (i == 5), 1 - i % 2, i % 2)
        return (rx + NX - d) % NX, half

    def load_u(i):
        src, half = piece(i)
        part = pl.ds((src * 2 + half) * (4 * PER), 4 * PER)
        return pltpu.make_async_copy(u_hbm.at[part], u.at[part], loc.at[1 + i])

    load_x = pltpu.make_async_copy(right_hbm, x, loc.at[9])
    load_x.start()

    def start_u(i, _):
        load_u(i).start()
        return 0

    lax.fori_loop(0, 8, start_u, 0)
    load_ur = pltpu.make_async_copy(upper_right_hbm, ur, loc.at[10])
    load_ur.start()
    load_ui = pltpu.make_async_copy(upper_inv_hbm, ui, loc.at[11])
    load_ui.start()

    barrier = pltpu.get_barrier_semaphore()
    peers = [off_x(1), off_x(3)] + [off_y(d) for d in range(1, NY)] + [off_z(d) for d in range(1, NZ)] + [sibling]
    for dev in peers:
        pl.semaphore_signal(barrier, inc=1, device_id=dev, device_id_type=MESH)

    lane = lax.broadcasted_iota(I32, (BLOCKS, W), 1)
    row = lax.broadcasted_iota(I32, (BLOCKS, W), 0)
    target = jnp.concatenate(
        [
            jnp.sum(jnp.where(lane[:W] == row[:W], target_ref[:, h * W : (h + 1) * W], 0), axis=1, keepdims=True)
            for h in range(BLOCKS // W)
        ],
        axis=0,
    )
    pos = jnp.sum(jnp.where(target == lane, place_ref[...], 0), axis=1, keepdims=True)
    cand = jnp.where(pos == lane, row, BLOCKS)
    for s in range(CAP):
        low = jnp.min(cand, axis=0, keepdims=True)
        idx_v[s : s + 1, :] = low
        cand = jnp.where(cand > low, cand, BLOCKS)
    where_in_g = (((pos // 2) % 2) * 2 + pos % 2) * (UPPER // 4) + ((pos // 4) % NZ) * NY + pos // (4 * NZ)
    for h in range(BLOCKS // W):
        idx_v[CAP + h : CAP + h + 1, :] = jnp.sum(jnp.where(row - h * W == lane, where_in_g, 0), axis=0, keepdims=True)
    idx_v[CAP + 2 :, :] = jnp.zeros((8 - CAP - 2, W), I32)
    to_smem = pltpu.make_async_copy(idx_v, idx_s, loc.at[12])
    to_smem.start()

    own.wait()
    lane16 = lax.broadcasted_iota(I32, (STRIP, W), 1)

    def strip(n, s):
        return inv[rx, n, s * STRIP : (s + 1) * STRIP, :].astype(F32)

    for h in range(2):
        for q in range(2):
            two = (h * 4 + q * 2, h * 4 + q * 2 + 1)
            for m, n in enumerate(two):
                for s in range(3):
                    pk[rx, h, q, m * 3 + s] = (strip(n, 6 - s) + pltpu.roll(strip(n, s), STRIP * (7 - s), 1)).astype(BF16)
                pk[rx, h, q, 6 + m] = inv[rx, n, 7 * STRIP :, :]
            pk[rx, h, q, 8] = (strip(two[0], 3) + pltpu.roll(strip(two[1], 3), W // 2, 1)).astype(BF16)

    pl.semaphore_wait(barrier, len(peers))

    mine_x = [pk.at[rx, 0], pk.at[rx, 1]]
    for h, i, d in ((0, 2, 1), (1, 3, 3), (1, 4, 1), (0, 5, 3)):
        send(mine_x[h], mine_x[h], xs.at[i], xr.at[i], off_x(d))
    relay_right, relay_left = pk.at[(rx + 3) % NX, 0], pk.at[(rx + 1) % NX, 1]
    relays = (
        remote(relay_right, relay_right, xs.at[6], xr.at[6], off_x(1)),
        remote(relay_left, relay_left, xs.at[7], xr.at[7], off_x(3)),
    )
    sends.extend(relays)
    t[BLOCKS] = jnp.zeros((COLS, W), F32)
    load_x.wait()

    def forward(i, _):
        src, half = piece(i)

        @pl.when(i >= 2)
        def _():
            arrived(pk.at[src, half], xs.at[i], xr.at[i], off_x(1))

            @pl.when(i == 2)
            def _():
                relays[0].start()

            @pl.when(i == 3)
            def _():
                relays[1].start()

            for q in range(2):
                for m in range(2):
                    n = half * 4 + q * 2 + m
                    for s in range(3):
                        both = pk[src, half, q, m * 3 + s].astype(F32)
                        cut = STRIP * (7 - s)
                        inv[src, n, (6 - s) * STRIP : (7 - s) * STRIP, :] = jnp.where(lane16 < cut, both, 0.0).astype(BF16)
                        inv[src, n, s * STRIP : (s + 1) * STRIP, :] = jnp.where(
                            lane16 < W - cut, pltpu.roll(both, W - cut, 1), 0.0
                        ).astype(BF16)
                    inv[src, n, 7 * STRIP :, :] = pk[src, half, q, 6 + m]
                    both = pk[src, half, q, 8].astype(F32)
                    if m:
                        both = pltpu.roll(both, W // 2, 1)
                    inv[src, n, 3 * STRIP : 4 * STRIP, :] = jnp.where(lane16 < W // 2, both, 0.0).astype(BF16)

        load_u(i).wait()
        base = src * GROUP + half * 4
        solved = []
        for q in range(4):
            f = lax.dot_general(x[base + q].astype(BF16), inv[src, half * 4 + q], NT, preferred_element_type=F32)
            lf[base + q] = f
            solved.append(f.astype(BF16))
        for q in range(4):
            n = base + q
            r = lax.dot_general(solved[q], u[pl.ds(n * PER, PER)].reshape(PER * W, W), NT, preferred_element_type=F32)
            for b in range(PER):
                t[n * PER + b] = r[:, b * W : (b + 1) * W]
        return 0

    lax.fori_loop(0, 8, forward, 0)
    to_smem.wait()

    def sum_of(p):
        return (t[idx_s[0, p]] + t[idx_s[1, p]]) + (t[idx_s[2, p]] + t[idx_s[3, p]])

    def at_z(d, yy, cc):
        return ((yy * NZ + (z + d) % NZ) * NC + cc) * 2

    def at_y(d, zz, cc):
        return ((((y + d) % NY) * NZ + zz) * NC + cc) * 2 + 1

    def sib_z(d):
        def body(k, _):
            az[d, k] = sum_of(at_z(d, k, 1 - c)).astype(BF16)
            return 0

        lax.fori_loop(0, NY, body, 0, unroll=True)
        send(az.at[d], bz.at[d], csz.at[d], crz.at[d], sibling)

    def sib_y(d):
        def body(k, _):
            ay[d, k] = sum_of(at_y(d, k, 1 - c)).astype(BF16)
            return 0

        lax.fori_loop(0, NZ, body, 0, unroll=4)
        send(ay.at[d], by.at[d], csy.at[d], cry.at[d], sibling)

    sib_z(4), sib_y(2), sib_z(3), sib_z(5), sib_y(1), sib_y(3)
    sib_z(2), sib_z(6), sib_z(1), sib_z(7), sib_y(0), sib_z(0)

    def has_z(d):
        arrived(bz.at[d], csz.at[d], crz.at[d], sibling)

    def has_y(d):
        arrived(by.at[d], csy.at[d], cry.at[d], sibling)

    def sum_z(d, k):
        return sum_of(at_z(d, k, c)) + bz[d, k].astype(F32)

    def sum_y(d, k):
        return sum_of(at_y(d, k, c)) + by[d, k].astype(F32)

    zr_dev, zl_dev, yr_dev, yl_dev = off_z(1), off_z(NZ - 1), off_y(1), off_y(NY - 1)

    has_z(4)
    for k in range(NY):
        oz[4, k] = sum_z(4, k).astype(BF16)
    lower, upper = pl.ds(0, 2), pl.ds(2, 2)
    send(oz.at[4, lower], rzr.at[0, lower], zs.at[0, 0], zr.at[0, 0], zr_dev)
    send(oz.at[4, upper], rzl.at[0, upper], zs.at[1, 0], zr.at[1, 0], zl_dev)
    has_y(2)

    def first_y(k, _):
        oy[2, k] = sum_y(2, k).astype(BF16)
        return 0

    lax.fori_loop(0, NZ, first_y, 0, unroll=4)
    low4, high4 = pl.ds(0, 4), pl.ds(4, 4)
    send(oy.at[2, low4], ryr.at[0, low4], ys.at[0, 0], yr.at[0, 0], yr_dev)
    send(oy.at[2, high4], ryl.at[0, high4], ys.at[1, 0], yr.at[1, 0], yl_dev)

    def z_step(s):
        for way, d, got, dev in ((0, 5 - s, rzr, zr_dev), (1, 3 + s, rzl, zl_dev)):
            has_z(d)
            part = got.at[s - 2] if s > 2 else got.at[0, lower if way == 0 else upper]
            arrived(part, zs.at[way, s - 2], zr.at[way, s - 2], dev)
            for k in range(NY):
                v = sum_z(d, k)
                if s > 2 or (k < 2) == (way == 0):
                    v = v + got[s - 2, k].astype(F32)
                oz[d, k] = v.astype(BF16)
            send(oz.at[d], got.at[s - 1], zs.at[way, s - 1], zr.at[way, s - 1], dev)

    z_step(2)
    for way, d, got, dev, part in ((0, 1, ryr, yr_dev, low4), (1, 3, ryl, yl_dev, high4)):
        has_y(d)
        arrived(got.at[0, part], ys.at[way, 0], yr.at[way, 0], dev)

        def with_got(k, _, d=d, got=got):
            oy[d, k] = (sum_y(d, k) + got[0, k].astype(F32)).astype(BF16)
            return 0

        def without(k, _, d=d):
            oy[d, k] = sum_y(d, k).astype(BF16)
            return 0

        for h in range(2):
            lax.fori_loop(4 * h, 4 * h + 4, with_got if h == way else without, 0, unroll=True)
        send(oy.at[d], got.at[1], ys.at[way, 1], yr.at[way, 1], dev)
    z_step(3)
    z_step(4)

    has_y(0)
    arrived(ryr.at[1], ys.at[0, 1], yr.at[0, 1], yr_dev)
    arrived(ryl.at[1], ys.at[1, 1], yr.at[1, 1], yl_dev)
    for d in (4, 3, 5, 2, 6, 1, 7, 0):
        k = (z + d) % NZ
        v = sum_y(0, k) + ryr[1, k].astype(F32) + ryl[1, k].astype(F32)
        if d:
            o2[d] = v.astype(BF16)
            send(o2.at[d], r2.at[d], s2.at[d], q2.at[d], off_z(d))
        else:
            keep[1] = v
    has_z(0)
    arrived(rzr.at[3], zs.at[0, 3], zr.at[0, 3], zr_dev)
    arrived(rzl.at[3], zs.at[1, 3], zr.at[1, 3], zl_dev)
    for d in (2, 1, 3, 0):
        k = (y + d) % NY
        v = sum_z(0, k) + rzr[3, k].astype(F32) + rzl[3, k].astype(F32)
        if d:
            o3[d] = v.astype(BF16)
            send(o3.at[d], r3.at[d], s3.at[d], q3.at[d], off_y(d))
        else:
            keep[0] = v
    load_ur.wait()
    load_ui.wait()

    def blk(j, zz, yy, n=1):
        return g.at[pl.ds((c * 2 + j) * (UPPER // 4) + ((zz + NZ) % NZ) * NY + (yy + NY) % NY, n)]

    def solve(j, total):
        v = (ur[j] - total).astype(BF16)
        h = lax.dot_general(v, ui[j], NT, preferred_element_type=F32).astype(BF16)
        s = lax.dot_general(h, ui[j], NN, preferred_element_type=F32)
        us[j] = s
        g[(c * 2 + j) * (UPPER // 4) + z * NY + y] = s.astype(BF16)

    def out1(d):
        b = blk(1, z - d, y)
        send(b, b, ays.at[0, d], ayr.at[0, d], yr_dev)
        send(b, b, ays.at[1, d], ayr.at[1, d], yl_dev)
        send(b, b, b1s.at[0, d], b1r.at[0, d], sibling)

    total = keep[1]
    for d in (1, 7, 2, 6, 3, 5, 4):
        arrived(r2.at[d], s2.at[d], q2.at[d], off_z(d))
        total = total + r2[d].astype(F32)
    solve(1, total)
    b = blk(1, z, y)
    for d in (4, 3, 5, 2, 6, 1, 7):
        send(b, b, azs.at[d], azr.at[d], off_z(d))
    out1(0)

    total = keep[0]
    for d in (1, 3, 2):
        arrived(r3.at[d], s3.at[d], q3.at[d], off_y(d))
        total = total + r3[d].astype(F32)
    solve(0, total)
    b = blk(0, z, y)
    for d in (2, 1, 3):
        send(b, b, aws.at[d], awr.at[d], off_y(d))
    store_us = pltpu.make_async_copy(us, upper_out, loc.at[13])
    store_us.start()

    def in1(d):
        b = blk(1, z - d, y)
        arrived(b, azs.at[d], azr.at[d], off_z(d))
        out1(d)

    halves = {0: 0, 1: 1, 7: 0, 2: 1, 6: 0, 3: 1, 5: 0, 4: 1}

    def along_y(d):
        for way, dy, dev in ((0, -1, yr_dev), (1, 1, yl_dev)):
            b = blk(1, z - d, y + dy)
            arrived(b, ays.at[way, d], ayr.at[way, d], dev)
            if halves[d] == way:
                send(b, b, ays.at[2, d], ayr.at[2, d], dev)
            send(b, b, b1s.at[1 + way, d], b1r.at[1 + way, d], sibling)

    def last_y(d):
        b = blk(1, z - d, y + 2)
        arrived(b, ays.at[2, d], ayr.at[2, d], yr_dev)
        send(b, b, b1s.at[3, d], b1r.at[3, d], sibling)

    def ring_piece(way, k):
        s = k // 2 + 1
        return blk(0, z - s if way == 0 else z + s, 2 * (k % 2 if way == 0 else 1 - k % 2), 2)

    def along_z(k):
        for way, dev in ((0, zr_dev), (1, zl_dev)):
            b = ring_piece(way, k)
            arrived(b, ars.at[way, k], arr.at[way, k], dev)
            if k <= 4:
                send(b, b, ars.at[way, k + 2], arr.at[way, k + 2], dev)
            send(b, b, b0s.at[way, k], b0r.at[way, k], sibling)

    for d in (1, 3, 2):
        b = blk(0, z, y - d)
        arrived(b, aws.at[d], awr.at[d], off_y(d))
    for k in range(2):
        for way, dev in ((0, zr_dev), (1, zl_dev)):
            b = blk(0, z, 2 * (k if way == 0 else 1 - k), 2)
            send(b, b, ars.at[way, k], arr.at[way, k], dev)
    b = blk(0, z, 0, NY)
    send(b, b, b0s.at[0, 7], b0r.at[0, 7], sibling)
    in1(1), in1(7), along_y(0), in1(2), in1(6), along_y(1), along_y(7)
    along_z(0), in1(3), in1(5), along_z(1), along_y(2), along_y(6), in1(4), along_z(2)
    along_y(3), along_y(5), along_z(3), along_y(4), along_z(4)
    for d in (0, 1, 7, 2, 6, 3, 5, 4):
        last_y(d)
    along_z(5), along_z(6)

    def there(j, zz, yy, n=1):
        return g.at[pl.ds(((1 - c) * 2 + j) * (UPPER // 4) + ((zz + NZ) % NZ) * NY + (yy + NY) % NY, n)]

    for d in range(NZ):
        for kind, dy in ((0, 0), (1, -1), (2, 1), (3, 2)):
            arrived(there(1, z - d, y + dy), b1s.at[kind, d], b1r.at[kind, d], sibling)
    arrived(there(0, z, 0, NY), b0s.at[0, 7], b0r.at[0, 7], sibling)
    for k in range(7):
        for way in range(2):
            s = k // 2 + 1
            b = there(0, z - s if way == 0 else z + s, 2 * (k % 2 if way == 0 else 1 - k % 2), 2)
            arrived(b, b0s.at[way, k], b0r.at[way, k], sibling)

    def backward(i, _):
        for q in range(4):
            n = i * 4 + q
            parts = []
            for b in range(PER):
                k = n * PER + b
                parts.append(g[idx_s[CAP + k // W, k % W]])
            corr = lax.dot_general(
                jnp.concatenate(parts, axis=1), u[pl.ds(n * PER, PER)].reshape(PER * W, W), NN, preferred_element_type=F32
            )
            back = (lf[n] - corr).astype(BF16)
            lo[n] = lax.dot_general(back, inv[n // GROUP, n % GROUP], NN, preferred_element_type=F32)
        return 0

    stores = []
    for i in range(4):
        lax.fori_loop(i * 2, i * 2 + 2, backward, 0)
        part = pl.ds(i * GROUP, GROUP)
        cp = pltpu.make_async_copy(lo.at[part], leaf_out.at[part], loc.at[14 + i])
        cp.start()
        stores.append(cp)
    for cp in sends:
        cp.wait_send()
    store_us.wait()
    for cp in stores:
        cp.wait()


def on_device(leaf_right, upper_right, leaf_inverse, upper_inverse, update_blocks, block_target, upper_place):
    any_space = pl.BlockSpec(memory_space=pl.ANY)
    vmem = pl.BlockSpec(memory_space=pltpu.VMEM)
    dma = pltpu.SemaphoreType.DMA
    leaves = NX * GROUP
    half = lambda *shape: pltpu.VMEM(shape + (COLS, W), BF16)
    wide = lambda *shape: pltpu.VMEM(shape + (COLS, W), F32)
    return pl.pallas_call(
        kernel,
        out_shape=(
            jax.ShapeDtypeStruct((leaves, COLS, W), F32),
            jax.ShapeDtypeStruct((2, COLS, W), F32),
        ),
        in_specs=[vmem, vmem] + [any_space] * 5,
        out_specs=(any_space, any_space),
        scratch_shapes=[
            pltpu.VMEM((BLOCKS, W, W), BF16),
            wide(leaves),
            pltpu.VMEM((NX, 2, 2, 9, STRIP, W), BF16),
            pltpu.VMEM((NX, GROUP, W, W), BF16),
            wide(leaves),
            wide(BLOCKS + 1),
            pltpu.VMEM((8, W), I32),
            pltpu.SMEM((8, W), I32),
            half(NZ, NY), half(NY, NZ),
            half(NZ, NY), half(NY, NZ),
            half(NZ, NY), half(NY, NZ),
            half(4, NY), half(4, NY),
            half(2, NZ), half(2, NZ),
            half(NZ), half(NZ),
            half(NY), half(NY),
            wide(2),
            wide(2),
            pltpu.VMEM((2, W, W), BF16),
            wide(2),
            half(UPPER),
            wide(leaves),
            dma((18,)),
            dma((8,)), dma((8,)),
            dma((NZ,)), dma((NZ,)), dma((NY,)), dma((NY,)),
            dma((2, 4)), dma((2, 4)), dma((2, 2)), dma((2, 2)),
            dma((NZ,)), dma((NZ,)), dma((NY,)), dma((NY,)),
            dma((NZ,)), dma((NZ,)),
            dma((3, NZ)), dma((3, NZ)),
            dma((NY,)), dma((NY,)),
            dma((2, 7)), dma((2, 7)),
            dma((4, NZ)), dma((4, NZ)),
            dma((2, 8)), dma((2, 8)),
        ],
        compiler_params=pltpu.CompilerParams(
            collective_id=0, has_side_effects=True, vmem_limit_bytes=56 * 2**20
        ),
        name="solve",
    )(block_target.reshape(1, -1), upper_place.reshape(1, -1), leaf_right, upper_right, leaf_inverse, upper_inverse, update_blocks)


def solution(mesh):
    return jax.shard_map(
        on_device,
        mesh=mesh,
        in_specs=(
            P("leaf", "rhs", None),
            P("leaf", "rhs", None),
            P(("leaf", "rhs"), None, None),
            P("leaf", None, None),
            P("leaf", None, None),
            P("leaf", None),
            P(),
        ),
        out_specs=(P("leaf", "rhs", None), P("leaf", "rhs", None)),
        check_vma=False,
    )
```

```python
import jax
import jax.numpy as jnp
from jax import lax
from jax.experimental import pallas as pl
from jax.experimental.pallas import tpu as pltpu
from jax.sharding import PartitionSpec as P

MESH = pl.DeviceIdType.MESH
F32, BF16, I32 = jnp.float32, jnp.bfloat16, jnp.int32
NX, NY, NZ, NC = 4, 4, 8, 2
PER = 8
GROUP = 8
COLS, W = 64, 128
BLOCKS = 256
CAP = 4
UPPER = NY * NZ * NC * 2
STRIP = 16
NT = (((1,), (1,)), ((), ()))
NN = (((1,), (0,)), ((), ()))


def kernel(
    target_ref, place_ref, right_hbm, upper_right_hbm, inv_hbm, upper_inv_hbm, u_hbm,
    lo, us,
    u, x, pk, inv, lf, t, idx_v, idx_s, az, ay, bz, by, oz, oy, rz, ry,
    o2, r2, o3, r3, keep, ur, ui, g,
    loc, xs, xr, csz, crz, csy, cry, zs, zr, ys, yr, s2, q2, s3, q3,
    azs, azr, ays, ayr, aws, awr, ars, arr, b1s, b1r, b0s, b0r, ready,
):
    leaf, rx = lax.axis_index("leaf"), lax.axis_index("rhs")
    y, z, c = leaf // (NZ * NC), (leaf // NC) % NZ, leaf % NC

    def at(yy, zz, cc, xx):
        return ((yy * NZ + zz) * NC + cc, xx)

    def off_x(d):
        return at(y, z, c, (rx + d) % NX)

    def off_y(d):
        return at((y + d) % NY, z, c, rx)

    def off_z(d):
        return at(y, (z + d) % NZ, c, rx)

    sibling = at(y, z, 1 - c, rx)
    sends = []

    def remote(src, dst, ssem, rsem, dev):
        return pltpu.make_async_remote_copy(
            src_ref=src, dst_ref=dst, send_sem=ssem, recv_sem=rsem, device_id=dev, device_id_type=MESH
        )

    def send(src, dst, ssem, rsem, dev):
        cp = remote(src, dst, ssem, rsem, dev)
        cp.start()
        sends.append(cp)

    def arrived(ref, ssem, rsem, dev):
        remote(ref, ref, ssem, rsem, dev).wait_recv()

    own = pltpu.make_async_copy(inv_hbm, inv.at[rx], loc.at[0])
    own.start()

    def pair_of(i, m):
        d = jnp.where(i < 2, 0, jnp.where(i >= 6, 2, 1 + 2 * (i % 2)))
        half = jnp.where(i >= 6, m, jnp.where((i == 4) | (i == 5), 1 - i % 2, i % 2))
        return (rx + NX - d) % NX, half, jnp.where(i >= 6, i % 2, m)

    def load_u(i, m):
        src, half, q = pair_of(i, m)
        part = pl.ds((src * 4 + half * 2 + q) * (2 * PER), 2 * PER)
        return pltpu.make_async_copy(u_hbm.at[part], u.at[part], loc.at[16 + 2 * i + m])

    load_x = pltpu.make_async_copy(right_hbm, x, loc.at[9])
    load_x.start()

    def start_u(i, _):
        load_u(i, 0).start()
        load_u(i, 1).start()
        return 0

    lax.fori_loop(0, 8, start_u, 0)
    load_ur = pltpu.make_async_copy(upper_right_hbm, ur, loc.at[10])
    load_ur.start()
    load_ui = pltpu.make_async_copy(upper_inv_hbm, ui, loc.at[11])
    load_ui.start()

    barrier = pltpu.get_barrier_semaphore()
    peers = [off_x(1), off_x(3)] + [off_y(1), off_y(3), off_z(1), off_z(7), sibling]
    for dev in peers:
        pl.semaphore_signal(barrier, inc=1, device_id=dev, device_id_type=MESH)

    lane = lax.broadcasted_iota(I32, (BLOCKS, W), 1)
    row = lax.broadcasted_iota(I32, (BLOCKS, W), 0)
    target = jnp.concatenate(
        [
            jnp.sum(jnp.where(lane[:W] == row[:W], target_ref[:, h * W : (h + 1) * W], 0), axis=1, keepdims=True)
            for h in range(BLOCKS // W)
        ],
        axis=0,
    )
    pos = jnp.sum(jnp.where(target == lane, place_ref[...], 0), axis=1, keepdims=True)
    cand = jnp.where(pos == lane, row, BLOCKS)
    for s in range(CAP):
        low = jnp.min(cand, axis=0, keepdims=True)
        idx_v[s : s + 1, :] = low
        cand = jnp.where(cand > low, cand, BLOCKS)
    where_in_g = (((pos // 2) % 2) * 2 + pos % 2) * (UPPER // 4) + ((pos // 4) % NZ) * NY + pos // (4 * NZ)
    for h in range(BLOCKS // W):
        idx_v[CAP + h : CAP + h + 1, :] = jnp.sum(jnp.where(row - h * W == lane, where_in_g, 0), axis=0, keepdims=True)
    idx_v[CAP + 2 :, :] = jnp.zeros((8 - CAP - 2, W), I32)
    to_smem = pltpu.make_async_copy(idx_v, idx_s, loc.at[12])
    to_smem.start()

    own.wait()
    lane16 = lax.broadcasted_iota(I32, (STRIP, W), 1)

    def strip(n, s):
        return inv[rx, n, s * STRIP : (s + 1) * STRIP, :].astype(F32)

    for h in range(2):
        for q in range(2):
            two = (h * 4 + q * 2, h * 4 + q * 2 + 1)
            for m, n in enumerate(two):
                for s in range(3):
                    pk[rx, h, q, m * 3 + s] = (strip(n, 6 - s) + pltpu.roll(strip(n, s), STRIP * (7 - s), 1)).astype(BF16)
                pk[rx, h, q, 6 + m] = inv[rx, n, 7 * STRIP :, :]
            pk[rx, h, q, 8] = (strip(two[0], 3) + pltpu.roll(strip(two[1], 3), W // 2, 1)).astype(BF16)

    pl.semaphore_wait(barrier, len(peers))

    def pass_on(i):
        for d in (1, NZ - 1):
            pl.semaphore_signal(ready.at[i], inc=1, device_id=off_z(d), device_id_type=MESH)

    pass_on(0)
    for d in (1, NY - 1):
        pl.semaphore_signal(ready.at[3], inc=1, device_id=off_y(d), device_id_type=MESH)

    for h, i, d in ((0, 2, 1), (1, 3, 3), (1, 4, 1), (0, 5, 3)):
        for q in range(2):
            b = pk.at[rx, h, q]
            send(b, b, xs.at[i, q], xr.at[i, q], off_x(d))
    relays = []
    for h, d in ((0, 1), (1, 3)):
        for q in range(2):
            b = pk.at[(rx + NX - d) % NX, h, q]
            relays.append(remote(b, b, xs.at[6 + q, h], xr.at[6 + q, h], off_x(d)))
    sends.extend(relays)
    t[BLOCKS] = jnp.zeros((COLS, W), F32)
    load_x.wait()

    def forward(i, _):
        @pl.when(i >= 2)
        def _():
            for m in range(2):
                src, half, q = pair_of(i, m)
                arrived(pk.at[src, half, q], xs.at[i, m], xr.at[i, m], off_x(1))
                for h in range(2):

                    @pl.when(i == 2 + h)
                    def _():
                        relays[2 * h + m].start()

            for k in range(2):

                @pl.when(i == 3 + 2 * k)
                def _():
                    pl.semaphore_wait(ready.at[k], 2)
                    pass_on(k + 1)

            for m in range(2):
                src, half, q = pair_of(i, m)
                for e in range(2):
                    n = half * 4 + q * 2 + e
                    for s in range(3):
                        both = pk[src, half, q, e * 3 + s].astype(F32)
                        cut = STRIP * (7 - s)
                        inv[src, n, (6 - s) * STRIP : (7 - s) * STRIP, :] = jnp.where(lane16 < cut, both, 0.0).astype(BF16)
                        inv[src, n, s * STRIP : (s + 1) * STRIP, :] = jnp.where(
                            lane16 < W - cut, pltpu.roll(both, W - cut, 1), 0.0
                        ).astype(BF16)
                    inv[src, n, 7 * STRIP :, :] = pk[src, half, q, 6 + e]
                    both = pk[src, half, q, 8].astype(F32)
                    if e:
                        both = pltpu.roll(both, W // 2, 1)
                    inv[src, n, 3 * STRIP : 4 * STRIP, :] = jnp.where(lane16 < W // 2, both, 0.0).astype(BF16)

        solved = []
        for m in range(2):
            src, half, q = pair_of(i, m)
            load_u(i, m).wait()
            for e in range(2):
                within = half * 4 + q * 2 + e
                n = src * GROUP + within
                f = lax.dot_general(x[n].astype(BF16), inv[src, within], NT, preferred_element_type=F32)
                lf[n] = f
                solved.append((n, f.astype(BF16)))
        for n, f in solved:
            r = lax.dot_general(f, u[pl.ds(n * PER, PER)].reshape(PER * W, W), NT, preferred_element_type=F32)
            for b in range(PER):
                t[n * PER + b] = r[:, b * W : (b + 1) * W]
        return 0

    lax.fori_loop(0, 8, forward, 0)
    to_smem.wait()
    pl.semaphore_wait(ready.at[2], 2)
    pl.semaphore_wait(ready.at[3], 2)

    def sum_of(p):
        return (t[idx_s[0, p]] + t[idx_s[1, p]]) + (t[idx_s[2, p]] + t[idx_s[3, p]])

    def at_z(d, yy, cc):
        return ((yy * NZ + (z + d) % NZ) * NC + cc) * 2

    def at_y(d, zz, cc):
        return ((((y + d) % NY) * NZ + zz) * NC + cc) * 2 + 1

    def sib_z(d):
        def body(k, _):
            az[d, k] = sum_of(at_z(d, k, 1 - c)).astype(BF16)
            return 0

        lax.fori_loop(0, NY, body, 0, unroll=True)
        send(az.at[d], bz.at[d], csz.at[d], crz.at[d], sibling)

    def sib_y(d):
        def body(k, _):
            ay[d, k] = sum_of(at_y(d, k, 1 - c)).astype(BF16)
            return 0

        lax.fori_loop(0, NZ, body, 0, unroll=4)
        send(ay.at[d], by.at[d], csy.at[d], cry.at[d], sibling)

    def has_z(d):
        arrived(bz.at[d], csz.at[d], crz.at[d], sibling)

    def has_y(d):
        arrived(by.at[d], csy.at[d], cry.at[d], sibling)

    def sum_z(d, k):
        return sum_of(at_z(d, k, c)) + bz[d, k].astype(F32)

    def sum_y(d, k):
        return sum_of(at_y(d, k, c)) + by[d, k].astype(F32)

    lower, upper = pl.ds(0, 2), pl.ds(2, 2)

    def own_z(d, more=()):
        has_z(d)
        for k in range(NY):
            v = sum_z(d, k)
            for got, used in more:
                if k in used:
                    v = v + rz[got, k].astype(F32)
            oz[d, k] = v.astype(BF16)

    def along(kind, d, way, to, part=None):
        a, b = oz.at[d], rz.at[way * 4 + kind]
        if part is not None:
            a, b = oz.at[d, part], rz.at[way * 4 + kind, part]
        send(a, b, zs.at[way, kind], zr.at[way, kind], off_z(to))

    def wait_z(kind, way, part=None):
        b = rz.at[way * 4 + kind] if part is None else rz.at[way * 4 + kind, part]
        arrived(b, zs.at[way, kind], zr.at[way, kind], off_z(1))

    def own_y(d):
        has_y(d)

        def body(k, _):
            oy[d, k] = sum_y(d, k).astype(BF16)
            return 0

        lax.fori_loop(0, NZ, body, 0, unroll=4)
        send(oy.at[d], ry.at[d], ys.at[d], yr.at[d], off_y(d))

    sib_z(3), sib_z(5), sib_z(4), sib_y(2)
    own_z(3)
    along(0, 3, 0, 1)
    own_z(5)
    along(0, 5, 1, 7)
    own_z(4)
    along(1, 4, 0, 2, lower)
    along(1, 4, 1, 6, upper)
    sib_y(1), sib_y(3)
    own_y(2)
    sib_z(1), sib_z(7)
    own_y(1), own_y(3)
    sib_z(2), sib_z(6)
    own_z(1)
    along(2, 1, 0, 1)
    own_z(7)
    along(2, 7, 1, 7)
    sib_y(0), sib_z(0)
    every = tuple(range(NY))
    wait_z(0, 0), wait_z(1, 0, lower)
    own_z(2, ((0, every), (1, (0, 1))))
    along(3, 2, 0, 2)
    wait_z(0, 1), wait_z(1, 1, upper)
    own_z(6, ((4, every), (5, (2, 3))))
    along(3, 6, 1, 6)

    has_y(0)
    for d in (1, 3, 2):
        arrived(ry.at[d], ys.at[d], yr.at[d], off_y(d))
    for d in (4, 3, 5, 2, 6, 1, 7, 0):
        k = (z + d) % NZ
        v = sum_y(0, k) + (ry[1, k].astype(F32) + ry[2, k].astype(F32)) + ry[3, k].astype(F32)
        if d:
            o2[d] = v.astype(BF16)
            send(o2.at[d], r2.at[d], s2.at[d], q2.at[d], off_z(d))
        else:
            keep[1] = v
    has_z(0)
    for way in range(2):
        wait_z(2, way), wait_z(3, way)
    for d in (2, 1, 3, 0):
        k = (y + d) % NY
        v = sum_z(0, k) + (rz[2, k].astype(F32) + rz[3, k].astype(F32)) + (rz[6, k].astype(F32) + rz[7, k].astype(F32))
        if d:
            o3[d] = v.astype(BF16)
            send(o3.at[d], r3.at[d], s3.at[d], q3.at[d], off_y(d))
        else:
            keep[0] = v
    load_ur.wait()
    load_ui.wait()

    def blk(j, zz, yy, n=1):
        return g.at[pl.ds((c * 2 + j) * (UPPER // 4) + ((zz + NZ) % NZ) * NY + (yy + NY) % NY, n)]

    def solve(j, total):
        v = (ur[j] - total).astype(BF16)
        h = lax.dot_general(v, ui[j], NT, preferred_element_type=F32).astype(BF16)
        s = lax.dot_general(h, ui[j], NN, preferred_element_type=F32)
        us[j] = s
        g[(c * 2 + j) * (UPPER // 4) + z * NY + y] = s.astype(BF16)

    def out1(d):
        b = blk(1, z - d, y)
        for dy in (2, 1, 3):
            send(b, b, ays.at[dy, d], ayr.at[dy, d], off_y(dy))
        send(b, b, b1s.at[0, d], b1r.at[0, d], sibling)

    n_sums = len(sends)
    total = keep[1]
    for d in (1, 7, 2, 6, 3, 5, 4):
        arrived(r2.at[d], s2.at[d], q2.at[d], off_z(d))
        total = total + r2[d].astype(F32)
    solve(1, total)
    b = blk(1, z, y)
    for d in (4, 3, 5, 2, 6, 1, 7):
        send(b, b, azs.at[d], azr.at[d], off_z(d))
    out1(0)

    total = keep[0]
    for d in (1, 3, 2):
        arrived(r3.at[d], s3.at[d], q3.at[d], off_y(d))
        total = total + r3[d].astype(F32)
    solve(0, total)
    b = blk(0, z, y)
    for d in (2, 1, 3):
        send(b, b, aws.at[d], awr.at[d], off_y(d))
    for cp in sends[:n_sums]:
        cp.wait_send()

    def in1(d):
        b = blk(1, z - d, y)
        arrived(b, azs.at[d], azr.at[d], off_z(d))
        out1(d)

    def along_y(d):
        for dy in (1, 3, 2):
            b = blk(1, z - d, y - dy)
            arrived(b, ays.at[dy, d], ayr.at[dy, d], off_y(dy))
            send(b, b, b1s.at[dy, d], b1r.at[dy, d], sibling)

    def ring_piece(way, k, mine=0):
        s, first = ((1, 0), (2, 1), (2, 0), (3, 1), (3, 0), (4, 1))[k]
        s = s - mine
        zz = z - s if way == 0 else z + s
        return (zz, 0, NY) if k == 0 else (zz, 2 * (1 - first if way == 0 else first), 2)

    def hop(way, n):
        return off_z(n if way == 0 else NZ - n)

    def along_z(k):
        for way in range(2):
            b = blk(0, *ring_piece(way, k))
            arrived(b, ars.at[way, k], arr.at[way, k], hop(way, 1))
            if k in (1, 2):
                send(b, b, ars.at[way, k + 2], arr.at[way, k + 2], hop(way, 1))
            if k == 1:
                send(b, b, ars.at[way, 5], arr.at[way, 5], hop(way, 2))
            send(b, b, b0s.at[way, k], b0r.at[way, k], sibling)

    in1(1), in1(7)
    for d in (1, 3, 2):
        b = blk(0, z, y - d)
        arrived(b, aws.at[d], awr.at[d], off_y(d))
    for k in (1, 2, 0):
        for way in range(2):
            b = blk(0, *ring_piece(way, k, 2 if k else 1))
            send(b, b, ars.at[way, k], arr.at[way, k], hop(way, 2 if k else 1))
    b = blk(0, z, 0, NY)
    send(b, b, b0s.at[0, 6], b0r.at[0, 6], sibling)
    in1(2), in1(6), along_y(0), in1(3), in1(5), in1(4)
    along_y(1), along_y(7), along_y(2), along_y(6), along_z(1), along_z(2)
    along_y(3), along_y(5), along_z(0), along_y(4), along_z(3), along_z(4), along_z(5)

    def there(j, zz, yy, n=1):
        return g.at[pl.ds(((1 - c) * 2 + j) * (UPPER // 4) + ((zz + NZ) % NZ) * NY + (yy + NY) % NY, n)]

    for d in range(NZ):
        for dy in range(NY):
            arrived(there(1, z - d, y - dy), b1s.at[dy, d], b1r.at[dy, d], sibling)
    arrived(there(0, z, 0, NY), b0s.at[0, 6], b0r.at[0, 6], sibling)
    for k in range(6):
        for way in range(2):
            arrived(there(0, *ring_piece(way, k)), b0s.at[way, k], b0r.at[way, k], sibling)

    def backward(i, _):
        backs = []
        for q in range(8):
            n = i * 8 + q
            parts = []
            for b in range(PER):
                k = n * PER + b
                parts.append(g[idx_s[CAP + k // W, k % W]])
            corr = lax.dot_general(
                jnp.concatenate(parts, axis=1), u[pl.ds(n * PER, PER)].reshape(PER * W, W), NN, preferred_element_type=F32
            )
            backs.append((lf[n] - corr).astype(BF16))
        for q in range(8):
            lo[i * 8 + q] = lax.dot_general(backs[q], inv[i, q], NN, preferred_element_type=F32)
        return 0

    lax.fori_loop(0, 4, backward, 0)
    for cp in sends[n_sums:]:
        cp.wait_send()


def on_device(leaf_right, upper_right, leaf_inverse, upper_inverse, update_blocks, block_target, upper_place):
    hbm = pl.BlockSpec(memory_space=pltpu.HBM)
    vmem = pl.BlockSpec(memory_space=pltpu.VMEM)
    dma = pltpu.SemaphoreType.DMA
    leaves = NX * GROUP
    half = lambda *shape: pltpu.VMEM(shape + (COLS, W), BF16)
    wide = lambda *shape: pltpu.VMEM(shape + (COLS, W), F32)
    return pl.pallas_call(
        kernel,
        out_shape=(pltpu.VMEM((leaves, COLS, W), F32), pltpu.VMEM((2, COLS, W), F32)),
        in_specs=[vmem, vmem] + [hbm] * 5,
        out_specs=(vmem, vmem),
        scratch_shapes=[
            pltpu.VMEM((BLOCKS, W, W), BF16),
            wide(leaves),
            pltpu.VMEM((NX, 2, 2, 9, STRIP, W), BF16),
            pltpu.VMEM((NX, GROUP, W, W), BF16),
            wide(leaves),
            wide(BLOCKS + 1),
            pltpu.VMEM((8, W), I32),
            pltpu.SMEM((8, W), I32),
            half(NZ, NY), half(NY, NZ),
            half(NZ, NY), half(NY, NZ),
            half(NZ, NY), half(NY, NZ),
            half(8, NY), half(NY, NZ),
            half(NZ), half(NZ),
            half(NY), half(NY),
            wide(2),
            wide(2),
            pltpu.VMEM((2, W, W), BF16),
            half(UPPER),
            dma((32,)),
            dma((8, 2)), dma((8, 2)),
            dma((NZ,)), dma((NZ,)), dma((NY,)), dma((NY,)),
            dma((2, 4)), dma((2, 4)), dma((NY,)), dma((NY,)),
            dma((NZ,)), dma((NZ,)), dma((NY,)), dma((NY,)),
            dma((NZ,)), dma((NZ,)),
            dma((NY, NZ)), dma((NY, NZ)),
            dma((NY,)), dma((NY,)),
            dma((2, 6)), dma((2, 6)),
            dma((4, NZ)), dma((4, NZ)),
            dma((2, 7)), dma((2, 7)),
            pltpu.SemaphoreType.REGULAR((4,)),
        ],
        compiler_params=pltpu.CompilerParams(
            collective_id=0, has_side_effects=True, vmem_limit_bytes=59 * 2**20
        ),
        name="solve",
    )(block_target.reshape(1, -1), upper_place.reshape(1, -1), leaf_right, upper_right, leaf_inverse, upper_inverse, update_blocks)


def solution(mesh):
    return jax.shard_map(
        on_device,
        mesh=mesh,
        in_specs=(
            P("leaf", "rhs", None),
            P("leaf", "rhs", None),
            P(("leaf", "rhs"), None, None),
            P("leaf", None, None),
            P("leaf", None, None),
            P("leaf", None),
            P(),
        ),
        out_specs=(P("leaf", "rhs", None), P("leaf", "rhs", None)),
        check_vma=False,
    )
```

```python
import jax
import jax.numpy as jnp
from jax import lax
from jax.experimental import pallas as pl
from jax.experimental.pallas import tpu as pltpu
from jax.sharding import PartitionSpec as P

MESH = pl.DeviceIdType.MESH
F32, BF16, I32 = jnp.float32, jnp.bfloat16, jnp.int32
NX, NY, NZ, NC = 4, 4, 8, 2
PER = 8
GROUP = 8
COLS, W = 64, 128
BLOCKS = 256
CAP = 4
UPPER = NY * NZ * NC * 2
STRIP = 16
NT = (((1,), (1,)), ((), ()))
NN = (((1,), (0,)), ((), ()))


def kernel(
    target_hbm, place_hbm, right_hbm, upper_right_hbm, inv_hbm, upper_inv_hbm, u_hbm,
    lo, us,
    target_ref, place_ref, u, x, pk, inv, lf, t, idx_v, idx_s, az, ay, bz, by, oz, oy, rz, ry,
    o2, r2, o3, r3, keep, ur, ui, g,
    loc, xr, crz, cry, zr, last_z, yr, q2, q3, azr, ayr, awr, arr, br,
    xs, csz, csy, zs, ys, s2, s3, gs, ready,
):
    leaf, rx = lax.axis_index("leaf"), lax.axis_index("rhs")
    y, z, c = leaf // (NZ * NC), (leaf // NC) % NZ, leaf % NC

    def at(yy, zz, cc, xx):
        return ((yy * NZ + zz) * NC + cc, xx)

    def off_x(d):
        return at(y, z, c, (rx + d) % NX)

    def off_y(d):
        return at((y + d) % NY, z, c, rx)

    def off_z(d):
        return at(y, (z + d) % NZ, c, rx)

    sibling = at(y, z, 1 - c, rx)

    def remote(src, dst, ssem, rsem, dev):
        return pltpu.make_async_remote_copy(
            src_ref=src, dst_ref=dst, send_sem=ssem, recv_sem=rsem, device_id=dev, device_id_type=MESH
        )

    def send(src, dst, ssem, rsem, dev):
        remote(src, dst, ssem, rsem, dev).start()

    def arrived(ref, rsem):
        remote(ref, ref, xs, rsem, sibling).wait_recv()

    def sent(ref, ssem):
        remote(ref, ref, ssem, br, sibling).wait_send()

    barrier = pltpu.get_barrier_semaphore()
    peers = [off_x(1), off_x(3)] + [off_y(1), off_y(3), off_z(1), off_z(7), sibling]
    for dev in peers:
        pl.semaphore_signal(barrier, inc=1, device_id=dev, device_id_type=MESH)

    own = pltpu.make_async_copy(inv_hbm, inv.at[rx], loc.at[0])
    own.start()
    load_target = pltpu.make_async_copy(target_hbm, target_ref, loc.at[5])
    load_target.start()
    load_place = pltpu.make_async_copy(place_hbm, place_ref, loc.at[6])
    load_place.start()

    def pair_of(i, m):
        d = jnp.where(i < 2, 0, jnp.where(i >= 6, 2, 1 + 2 * (i % 2)))
        half = jnp.where(i >= 6, m, jnp.where((i == 4) | (i == 5), 1 - i % 2, i % 2))
        return (rx + NX - d) % NX, half, jnp.where(i >= 6, i % 2, m)

    def load_u(i, m):
        src, half, q = pair_of(i, m)
        part = pl.ds((src * 4 + half * 2 + q) * (2 * PER), 2 * PER)
        return pltpu.make_async_copy(u_hbm.at[part], u.at[part], loc.at[7 + i])

    load_x = pltpu.make_async_copy(right_hbm, x, loc.at[1])
    load_x.start()

    def start_u(i, _):
        load_u(i, 0).start()
        load_u(i, 1).start()
        return 0

    lax.fori_loop(0, 8, start_u, 0)
    load_ur = pltpu.make_async_copy(upper_right_hbm, ur, loc.at[2])
    load_ur.start()
    load_ui = pltpu.make_async_copy(upper_inv_hbm, ui, loc.at[3])
    load_ui.start()

    own.wait()
    lane16 = lax.broadcasted_iota(I32, (STRIP, W), 1)

    def strip(n, s):
        return inv[rx, n, s * STRIP : (s + 1) * STRIP, :].astype(F32)

    for h in range(2):
        for q in range(2):
            two = (h * 4 + q * 2, h * 4 + q * 2 + 1)
            for m, n in enumerate(two):
                for s in range(3):
                    pk[rx, h, q, m * 3 + s] = (strip(n, 6 - s) + pltpu.roll(strip(n, s), STRIP * (7 - s), 1)).astype(BF16)
                pk[rx, h, q, 6 + m] = inv[rx, n, 7 * STRIP :, :]
            pk[rx, h, q, 8] = (strip(two[0], 3) + pltpu.roll(strip(two[1], 3), W // 2, 1)).astype(BF16)

    pl.semaphore_wait(barrier, len(peers))

    def pass_on(i, near):
        for d in (near, NZ - near):
            pl.semaphore_signal(ready.at[i], inc=1, device_id=off_z(d), device_id_type=MESH)

    pass_on(0, 1)
    for d in (1, NY - 1):
        pl.semaphore_signal(ready.at[2], inc=1, device_id=off_y(d), device_id_type=MESH)

    for h, i, d in ((0, 2, 1), (1, 3, 3), (1, 4, 1), (0, 5, 3)):
        for q in range(2):
            b = pk.at[rx, h, q]
            send(b, b, xs, xr.at[i - 2, q], off_x(d))
    relays = []
    for h, d in ((0, 1), (1, 3)):
        for q in range(2):
            b = pk.at[(rx + NX - d) % NX, h, q]
            relays.append(remote(b, b, xs, xr.at[4 + q, h], off_x(d)))
    load_target.wait()
    load_place.wait()
    lane = lax.broadcasted_iota(I32, (BLOCKS, W), 1)
    row = lax.broadcasted_iota(I32, (BLOCKS, W), 0)
    target = jnp.concatenate(
        [
            jnp.sum(jnp.where(lane[:W] == row[:W], target_ref[:, h * W : (h + 1) * W], 0), axis=1, keepdims=True)
            for h in range(BLOCKS // W)
        ],
        axis=0,
    )
    pos = jnp.sum(jnp.where(target == lane, place_ref[...], 0), axis=1, keepdims=True)
    cand = jnp.where(pos == lane, row, BLOCKS)
    for s in range(CAP):
        low = jnp.min(cand, axis=0, keepdims=True)
        idx_v[s : s + 1, :] = low
        cand = jnp.where(cand > low, cand, BLOCKS)
    where_in_g = (((pos // 2) % 2) * 2 + pos % 2) * (UPPER // 4) + ((pos // 4) % NZ) * NY + pos // (4 * NZ)
    for h in range(BLOCKS // W):
        idx_v[CAP + h : CAP + h + 1, :] = jnp.sum(jnp.where(row - h * W == lane, where_in_g, 0), axis=0, keepdims=True)
    idx_v[CAP + 2 :, :] = jnp.zeros((8 - CAP - 2, W), I32)
    to_smem = pltpu.make_async_copy(idx_v, idx_s, loc.at[4])
    to_smem.start()

    t[BLOCKS] = jnp.zeros((COLS, W), F32)
    load_x.wait()

    def forward(i, _):
        @pl.when(i == 2)
        def _():
            pl.semaphore_wait(ready.at[0], 2)
            pass_on(1, 2)

        @pl.when(i >= 2)
        def _():
            for m in range(2):
                src, half, q = pair_of(i, m)
                arrived(pk.at[src, half, q], xr.at[i - 2, m])
                for h in range(2):

                    @pl.when(i == 2 + h)
                    def _():
                        relays[2 * h + m].start()

            for m in range(2):
                src, half, q = pair_of(i, m)
                for e in range(2):
                    n = half * 4 + q * 2 + e
                    for s in range(3):
                        both = pk[src, half, q, e * 3 + s].astype(F32)
                        cut = STRIP * (7 - s)
                        inv[src, n, (6 - s) * STRIP : (7 - s) * STRIP, :] = jnp.where(lane16 < cut, both, 0.0).astype(BF16)
                        inv[src, n, s * STRIP : (s + 1) * STRIP, :] = jnp.where(
                            lane16 < W - cut, pltpu.roll(both, W - cut, 1), 0.0
                        ).astype(BF16)
                    inv[src, n, 7 * STRIP :, :] = pk[src, half, q, 6 + e]
                    both = pk[src, half, q, 8].astype(F32)
                    if e:
                        both = pltpu.roll(both, W // 2, 1)
                    inv[src, n, 3 * STRIP : 4 * STRIP, :] = jnp.where(lane16 < W // 2, both, 0.0).astype(BF16)

        some = u.at[pl.ds(0, 4 * PER)]
        pltpu.make_async_copy(some, some, loc.at[7 + i]).wait()
        solved = []
        for m in range(2):
            src, half, q = pair_of(i, m)
            for e in range(2):
                within = half * 4 + q * 2 + e
                n = src * GROUP + within
                f = lax.dot_general(x[n].astype(BF16), inv[src, within], NT, preferred_element_type=F32)
                lf[n] = f
                solved.append((n, f.astype(BF16)))
        for n, f in solved:
            r = lax.dot_general(f, u[pl.ds(n * PER, PER)].reshape(PER * W, W), NT, preferred_element_type=F32)
            for b in range(PER):
                t[n * PER + b] = r[:, b * W : (b + 1) * W]
        return 0

    lax.fori_loop(0, 8, forward, 0)
    to_smem.wait()
    pl.semaphore_wait(ready.at[1], 2)
    pl.semaphore_wait(ready.at[2], 2)

    def sum_of(p):
        return (t[idx_s[0, p]] + t[idx_s[1, p]]) + (t[idx_s[2, p]] + t[idx_s[3, p]])

    def at_z(d, yy, cc):
        return ((yy * NZ + (z + d) % NZ) * NC + cc) * 2

    z_order = (4, 3, 5, 2, 6, 1, 7, 0)

    def at_y(d, k, cc):
        return ((((y + d) % NY) * NZ + (z + z_order[k]) % NZ) * NC + cc) * 2 + 1

    def sib_z(d):
        sums = [sum_of(at_z(d, k, 1 - c)).astype(BF16) for k in range(NY)]
        for k in range(NY):
            az[d, k] = sums[k]
        send(az.at[d], bz.at[d], csz, crz.at[d], sibling)

    def sib_y(d):
        for h in range(0, NZ, 4):
            sums = [sum_of(at_y(d, h + k, 1 - c)).astype(BF16) for k in range(4)]
            for k in range(4):
                ay[d, h + k] = sums[k]
        send(ay.at[d], by.at[d], csy, cry.at[d], sibling)

    def has_z(d):
        arrived(bz.at[d], crz.at[d])

    def has_y(d):
        arrived(by.at[d], cry.at[d])

    def sum_z(d, k):
        return sum_of(at_z(d, k, c)) + bz[d, k].astype(F32)

    def sum_y(d, k):
        return sum_of(at_y(d, k, c)) + by[d, k].astype(F32)

    lower, upper = pl.ds(0, 2), pl.ds(2, 2)

    def own_z(d, part, more=()):
        sums = []
        for k in part:
            v = sum_z(d, k)
            for got in more:
                v = v + rz[got, k].astype(F32)
            sums.append(v.astype(BF16))
        for k, v in zip(part, sums):
            oz[d, k] = v

    def along(kind, d, way, to, part, sem):
        here = pl.ds(part[0], len(part))
        send(oz.at[d, here], rz.at[way * 4 + kind, here], zs, sem, off_z(to if way == 0 else NZ - to))

    def wait_z(kind, way, part, sem):
        arrived(rz.at[way * 4 + kind, pl.ds(part[0], len(part))], sem)

    def own_y(d, h):
        sums = [sum_y(d, h + k).astype(BF16) for k in range(4)]
        for k in range(4):
            oy[d, h + k] = sums[k]
        here = pl.ds(h, 4)
        send(oy.at[d, here], ry.at[d, here], ys, yr.at[h // 4], off_y(d))

    lower, upper, every = (0, 1), (2, 3), (0, 1, 2, 3)
    firsts, seconds = (lower, upper), (upper, lower)
    sib_z(4), sib_z(3), sib_z(5), sib_y(2)
    has_z(4)
    own_z(4, every)
    for way in range(2):
        along(1, 4, way, 2, firsts[way], zr.at[way, 0])
    for way, d in ((0, 3), (1, 5)):
        has_z(d)
        own_z(d, every)
        along(0, d, way, 1, firsts[way], zr.at[way, 1])
    for way, d in ((0, 3), (1, 5)):
        along(0, d, way, 1, seconds[way], zr.at[way, 2])
    sib_y(1), sib_y(3), sib_z(1), sib_z(7)
    has_y(2)
    own_y(2, 0)
    has_y(1)
    own_y(1, 0)
    has_y(3)
    own_y(3, 0)
    for d in (2, 1, 3):
        own_y(d, 4)
    for way, d in ((0, 1), (1, 7)):
        has_z(d)
        own_z(d, every)
        along(2, d, way, 1, every, last_z)
    sib_z(2), sib_z(6), sib_y(0), sib_z(0)
    for way, d in ((0, 2), (1, 6)):
        has_z(d)
        wait_z(1, way, firsts[way], zr.at[way, 0])
        wait_z(0, way, firsts[way], zr.at[way, 1])
        own_z(d, firsts[way], (way * 4, way * 4 + 1))
        along(3, d, way, 2, firsts[way], last_z)
    for way, d in ((0, 2), (1, 6)):
        wait_z(0, way, seconds[way], zr.at[way, 2])
        own_z(d, seconds[way], (way * 4,))
        along(3, d, way, 2, seconds[way], last_z)

    has_y(0)
    for h in range(2):
        arrived(ry.at[pl.ds(1, 3), pl.ds(4 * h, 4)], yr.at[h])
        for k in range(4 * h, 4 * h + 4):
            d = z_order[k]
            v = sum_y(0, k) + (ry[1, k].astype(F32) + ry[2, k].astype(F32)) + ry[3, k].astype(F32)
            if d:
                o2[d] = v.astype(BF16)
                send(o2.at[d], r2.at[d], s2, q2, off_z(d))
            else:
                keep[1] = v
    has_z(0)
    arrived(rz.at[pl.ds(0, 4)], last_z)
    for d in (2, 1, 3, 0):
        k = (y + d) % NY
        v = sum_z(0, k) + (rz[2, k].astype(F32) + rz[3, k].astype(F32)) + (rz[6, k].astype(F32) + rz[7, k].astype(F32))
        if d:
            o3[d] = v.astype(BF16)
            send(o3.at[d], r3.at[d], s3, q3, off_y(d))
        else:
            keep[0] = v
    load_ur.wait()
    load_ui.wait()

    def blk(j, zz, yy, n=1):
        return g.at[pl.ds((c * 2 + j) * (UPPER // 4) + ((zz + NZ) % NZ) * NY + (yy + NY) % NY, n)]

    def solve(j, total):
        v = (ur[j] - total).astype(BF16)
        h = lax.dot_general(v, ui[j], NT, preferred_element_type=F32).astype(BF16)
        s = lax.dot_general(h, ui[j], NN, preferred_element_type=F32)
        us[j] = s
        g[(c * 2 + j) * (UPPER // 4) + z * NY + y] = s.astype(BF16)

    def out1(d):
        b = blk(1, z - d, y)
        for dy in (2, 1, 3):
            send(b, b, gs, ayr.at[d], off_y(dy))
        send(b, b, gs, br, sibling)

    total = keep[1]
    arrived(r2.at[pl.ds(1, NZ - 1)], q2)
    for d in range(1, NZ):
        total = total + r2[d].astype(F32)
    solve(1, total)
    b = blk(1, z, y)
    for d in (4, 3, 5, 2, 6, 1, 7):
        send(b, b, gs, azr.at[d], off_z(d))
    out1(0)

    total = keep[0]
    arrived(r3.at[pl.ds(1, NY - 1)], q3)
    for d in range(1, NY):
        total = total + r3[d].astype(F32)
    solve(0, total)
    b = blk(0, z, y)
    for d in (2, 1, 3):
        send(b, b, gs, awr, off_y(d))

    def in1(d):
        arrived(blk(1, z - d, y), azr.at[d])
        out1(d)

    def along_y(d):
        arrived(g.at[pl.ds(0, NY - 1)], ayr.at[d])
        for dy in (1, 3, 2):
            b = blk(1, z - d, y - dy)
            send(b, b, gs, br, sibling)

    def ring_piece(way, k, mine=0):
        s, first = ((1, 0), (2, 1), (2, 0), (3, 1), (3, 0), (4, 1))[k]
        s = s - mine
        zz = z - s if way == 0 else z + s
        return (zz, 0, NY) if k == 0 else (zz, 2 * (1 - first if way == 0 else first), 2)

    def hop(way, n):
        return off_z(n if way == 0 else NZ - n)

    def along_z(k):
        for way in range(2):
            b = blk(0, *ring_piece(way, k))
            arrived(b, arr.at[way, k])
            if k in (1, 2):
                send(b, b, gs, arr.at[way, k + 2], hop(way, 1))
            if k == 1:
                send(b, b, gs, arr.at[way, 5], hop(way, 2))
            send(b, b, gs, br, sibling)

    in1(1), in1(7)
    arrived(g.at[pl.ds(0, NY - 1)], awr)
    for k in (1, 2, 0):
        for way in range(2):
            b = blk(0, *ring_piece(way, k, 2 if k else 1))
            send(b, b, gs, arr.at[way, k], hop(way, 2 if k else 1))
    b = blk(0, z, 0, NY)
    send(b, b, gs, br, sibling)
    in1(2), in1(6), along_y(0), in1(3), in1(5), in1(4)
    along_y(1), along_y(7), along_y(2), along_y(6), along_z(1), along_z(2)
    along_y(3), along_y(5), along_z(0), along_y(4), along_z(3), along_z(4), along_z(5)
    arrived(g.at[pl.ds(0, UPPER // 2)], br)

    def backward(i, _):
        backs = []
        for q in range(8):
            n = i * 8 + q
            parts = []
            for b in range(PER):
                k = n * PER + b
                parts.append(g[idx_s[CAP + k // W, k % W]])
            corr = lax.dot_general(
                jnp.concatenate(parts, axis=1), u[pl.ds(n * PER, PER)].reshape(PER * W, W), NN, preferred_element_type=F32
            )
            backs.append((lf[n] - corr).astype(BF16))
        for q in range(8):
            lo[i * 8 + q] = lax.dot_general(backs[q], inv[i, q], NN, preferred_element_type=F32)
        return 0

    lax.fori_loop(0, 4, backward, 0)
    sent(pk.at[pl.ds(0, 3)], xs)
    sent(az, csz)
    sent(ay, csy)
    sent(oz.at[pl.ds(0, 7)], zs)
    sent(oy.at[pl.ds(0, 3)], ys)
    sent(o2.at[pl.ds(0, NZ - 1)], s2)
    sent(o3.at[pl.ds(0, NY - 1)], s3)
    sent(g.at[pl.ds(0, 126)], gs)


def on_device(leaf_right, upper_right, leaf_inverse, upper_inverse, update_blocks, block_target, upper_place):
    hbm = pl.BlockSpec(memory_space=pltpu.HBM)
    vmem = pl.BlockSpec(memory_space=pltpu.VMEM)
    dma = pltpu.SemaphoreType.DMA
    leaves = NX * GROUP
    half = lambda *shape: pltpu.VMEM(shape + (COLS, W), BF16)
    wide = lambda *shape: pltpu.VMEM(shape + (COLS, W), F32)
    return pl.pallas_call(
        kernel,
        out_shape=(pltpu.VMEM((leaves, COLS, W), F32), pltpu.VMEM((2, COLS, W), F32)),
        in_specs=[hbm] * 7,
        out_specs=(vmem, vmem),
        scratch_shapes=[
            pltpu.VMEM((1, BLOCKS), I32),
            pltpu.VMEM((1, W), I32),
            pltpu.VMEM((BLOCKS, W, W), BF16),
            wide(leaves),
            pltpu.VMEM((NX, 2, 2, 9, STRIP, W), BF16),
            pltpu.VMEM((NX, GROUP, W, W), BF16),
            wide(leaves),
            wide(BLOCKS + 1),
            pltpu.VMEM((8, W), I32),
            pltpu.SMEM((8, W), I32),
            half(NZ, NY), half(NY, NZ),
            half(NZ, NY), half(NY, NZ),
            half(NZ, NY), half(NY, NZ),
            half(8, NY), half(NY, NZ),
            half(NZ), half(NZ),
            half(NY), half(NY),
            wide(2),
            wide(2),
            pltpu.VMEM((2, W, W), BF16),
            half(UPPER),
            dma((15,)),
            dma((6, 2)),
            dma((NZ,)), dma((NY,)),
            dma((2, 3)), dma, dma((2,)),
            dma, dma,
            dma((NZ,)), dma((NZ,)), dma, dma((2, 6)), dma,
            dma, dma, dma, dma, dma, dma, dma, dma,
            pltpu.SemaphoreType.REGULAR((3,)),
        ],
        compiler_params=pltpu.CompilerParams(
            collective_id=0, has_side_effects=True, vmem_limit_bytes=59 * 2**20
        ),
        name="solve",
    )(block_target.reshape(1, -1), upper_place.reshape(1, -1), leaf_right, upper_right, leaf_inverse, upper_inverse, update_blocks)


def solution(mesh):
    return jax.shard_map(
        on_device,
        mesh=mesh,
        in_specs=(
            P("leaf", "rhs", None),
            P("leaf", "rhs", None),
            P(("leaf", "rhs"), None, None),
            P("leaf", None, None),
            P("leaf", None, None),
            P("leaf", None),
            P(),
        ),
        out_specs=(P("leaf", "rhs", None), P("leaf", "rhs", None)),
        check_vma=False,
    )
```

```python
import jax
import jax.numpy as jnp
from jax import lax
from jax.experimental import pallas as pl
from jax.experimental.pallas import tpu as pltpu
from jax.sharding import PartitionSpec as P

MESH = pl.DeviceIdType.MESH
F32, BF16, I32 = jnp.float32, jnp.bfloat16, jnp.int32
NX, NY, NZ, NC = 4, 4, 8, 2
PER = 8
GROUP = 8
COLS, W = 64, 128
BLOCKS = 256
CAP = 4
UPPER = NY * NZ * NC * 2
STRIP = 16
NT = (((1,), (1,)), ((), ()))
NN = (((1,), (0,)), ((), ()))


def kernel(
    target_hbm, place_hbm, right_hbm, upper_right_hbm, inv_hbm, upper_inv_hbm, u_hbm,
    lo, us,
    target_ref, place_ref, u, x, pk, inv, lf, t, idx_v, idx_s, az, ay, bz, by, oz, oy, rz, ry,
    o2, r2, r3, keep, ur, ui, ur1, ui1, solved_y, g,
    loc, xr, crz, cry, zr, last_z, yr, q2, q3, azr, ayr, arr, br, mr,
    xs, csz, csy, zs, ys, s2, s3, gs, ms, ready,
):
    leaf, rx = lax.axis_index("leaf"), lax.axis_index("rhs")
    y, z, c = leaf // (NZ * NC), (leaf // NC) % NZ, leaf % NC

    def at(yy, zz, cc, xx):
        return ((yy * NZ + zz) * NC + cc, xx)

    def off_x(d):
        return at(y, z, c, (rx + d) % NX)

    def off_y(d):
        return at((y + d) % NY, z, c, rx)

    def off_z(d):
        return at(y, (z + d) % NZ, c, rx)

    sibling = at(y, z, 1 - c, rx)

    def remote(src, dst, ssem, rsem, dev):
        return pltpu.make_async_remote_copy(
            src_ref=src, dst_ref=dst, send_sem=ssem, recv_sem=rsem, device_id=dev, device_id_type=MESH
        )

    def send(src, dst, ssem, rsem, dev):
        remote(src, dst, ssem, rsem, dev).start()

    def arrived(ref, rsem):
        remote(ref, ref, xs, rsem, sibling).wait_recv()

    def sent(ref, ssem):
        remote(ref, ref, ssem, br, sibling).wait_send()

    barrier = pltpu.get_barrier_semaphore()
    peers = [off_x(1), off_x(3)] + [off_y(1), off_y(3), off_z(1), off_z(7), sibling]
    for dev in peers:
        pl.semaphore_signal(barrier, inc=1, device_id=dev, device_id_type=MESH)

    own = pltpu.make_async_copy(inv_hbm, inv.at[rx], loc.at[0])
    own.start()
    load_target = pltpu.make_async_copy(target_hbm, target_ref, loc.at[5])
    load_target.start()
    load_place = pltpu.make_async_copy(place_hbm, place_ref, loc.at[6])
    load_place.start()

    def pair_of(i, m):
        d = jnp.where(i < 2, 0, jnp.where(i >= 6, 2, 1 + 2 * (i % 2)))
        half = jnp.where(i >= 6, m, jnp.where((i == 4) | (i == 5), 1 - i % 2, i % 2))
        return (rx + NX - d) % NX, half, jnp.where(i >= 6, i % 2, m)

    def load_u(i, m):
        src, half, q = pair_of(i, m)
        part = pl.ds((src * 4 + half * 2 + q) * (2 * PER), 2 * PER)
        return pltpu.make_async_copy(u_hbm.at[part], u.at[part], loc.at[7 + i])

    load_x = pltpu.make_async_copy(right_hbm, x, loc.at[1])
    load_x.start()

    def start_u(i, _):
        load_u(i, 0).start()
        load_u(i, 1).start()
        return 0

    lax.fori_loop(0, 8, start_u, 0)
    uppers = [
        pltpu.make_async_copy(upper_right_hbm.at[0], ur.at[y], loc.at[2]),
        pltpu.make_async_copy(upper_right_hbm.at[1], ur1, loc.at[3]),
        pltpu.make_async_copy(upper_inv_hbm.at[0], ui.at[y], loc.at[15]),
        pltpu.make_async_copy(upper_inv_hbm.at[1], ui1, loc.at[16]),
    ]
    for cp in uppers:
        cp.start()

    own.wait()
    lane16 = lax.broadcasted_iota(I32, (STRIP, W), 1)

    def strip(n, s):
        return inv[rx, n, s * STRIP : (s + 1) * STRIP, :].astype(F32)

    for h in range(2):
        for q in range(2):
            two = (h * 4 + q * 2, h * 4 + q * 2 + 1)
            for m, n in enumerate(two):
                for s in range(3):
                    pk[rx, h, q, m * 3 + s] = (strip(n, 6 - s) + pltpu.roll(strip(n, s), STRIP * (7 - s), 1)).astype(BF16)
                pk[rx, h, q, 6 + m] = inv[rx, n, 7 * STRIP :, :]
            pk[rx, h, q, 8] = (strip(two[0], 3) + pltpu.roll(strip(two[1], 3), W // 2, 1)).astype(BF16)

    pl.semaphore_wait(barrier, len(peers))

    def pass_on(i, near):
        for d in (near, NZ - near):
            pl.semaphore_signal(ready.at[i], inc=1, device_id=off_z(d), device_id_type=MESH)

    pass_on(0, 1)
    for d in (1, NY - 1):
        pl.semaphore_signal(ready.at[2], inc=1, device_id=off_y(d), device_id_type=MESH)

    for h, i, d in ((0, 2, 1), (1, 3, 3), (1, 4, 1), (0, 5, 3)):
        for q in range(2):
            b = pk.at[rx, h, q]
            send(b, b, xs, xr.at[i - 2, q], off_x(d))
    relays = []
    for h, d in ((0, 1), (1, 3)):
        for q in range(2):
            b = pk.at[(rx + NX - d) % NX, h, q]
            relays.append(remote(b, b, xs, xr.at[4 + q, h], off_x(d)))
    load_target.wait()
    load_place.wait()
    lane = lax.broadcasted_iota(I32, (BLOCKS, W), 1)
    row = lax.broadcasted_iota(I32, (BLOCKS, W), 0)
    target = jnp.concatenate(
        [
            jnp.sum(jnp.where(lane[:W] == row[:W], target_ref[:, h * W : (h + 1) * W], 0), axis=1, keepdims=True)
            for h in range(BLOCKS // W)
        ],
        axis=0,
    )
    pos = jnp.sum(jnp.where(target == lane, place_ref[...], 0), axis=1, keepdims=True)
    cand = jnp.where(pos == lane, row, BLOCKS)
    for s in range(CAP):
        low = jnp.min(cand, axis=0, keepdims=True)
        idx_v[s : s + 1, :] = low
        cand = jnp.where(cand > low, cand, BLOCKS)
    where_in_g = (((pos // 2) % 2) * 2 + pos % 2) * (UPPER // 4) + ((pos // 4) % NZ) * NY + pos // (4 * NZ)
    for h in range(BLOCKS // W):
        idx_v[CAP + h : CAP + h + 1, :] = jnp.sum(jnp.where(row - h * W == lane, where_in_g, 0), axis=0, keepdims=True)
    idx_v[CAP + 2 :, :] = jnp.zeros((8 - CAP - 2, W), I32)
    to_smem = pltpu.make_async_copy(idx_v, idx_s, loc.at[4])
    to_smem.start()

    t[BLOCKS] = jnp.zeros((COLS, W), F32)
    load_x.wait()

    def forward(i, _):
        @pl.when(i == 2)
        def _():
            pl.semaphore_wait(ready.at[0], 2)
            pass_on(1, 2)

        @pl.when(i == 4)
        def _():
            for cp in uppers:
                cp.wait()
            pl.semaphore_wait(ready.at[2], 2)
            for d in (2, 1, 3):
                send(ui.at[y], ui.at[y], ms.at[0], mr.at[0], off_y(d))
                send(ur.at[y], ur.at[y], ms.at[1], mr.at[1], off_y(d))

        @pl.when(i >= 2)
        def _():
            for m in range(2):
                src, half, q = pair_of(i, m)
                arrived(pk.at[src, half, q], xr.at[i - 2, m])
                for h in range(2):

                    @pl.when(i == 2 + h)
                    def _():
                        relays[2 * h + m].start()

            for m in range(2):
                src, half, q = pair_of(i, m)
                for e in range(2):
                    n = half * 4 + q * 2 + e
                    for s in range(3):
                        both = pk[src, half, q, e * 3 + s].astype(F32)
                        cut = STRIP * (7 - s)
                        inv[src, n, (6 - s) * STRIP : (7 - s) * STRIP, :] = jnp.where(lane16 < cut, both, 0.0).astype(BF16)
                        inv[src, n, s * STRIP : (s + 1) * STRIP, :] = jnp.where(
                            lane16 < W - cut, pltpu.roll(both, W - cut, 1), 0.0
                        ).astype(BF16)
                    inv[src, n, 7 * STRIP :, :] = pk[src, half, q, 6 + e]
                    both = pk[src, half, q, 8].astype(F32)
                    if e:
                        both = pltpu.roll(both, W // 2, 1)
                    inv[src, n, 3 * STRIP : 4 * STRIP, :] = jnp.where(lane16 < W // 2, both, 0.0).astype(BF16)

        some = u.at[pl.ds(0, 4 * PER)]
        pltpu.make_async_copy(some, some, loc.at[7 + i]).wait()
        solved = []
        for m in range(2):
            src, half, q = pair_of(i, m)
            for e in range(2):
                within = half * 4 + q * 2 + e
                n = src * GROUP + within
                f = lax.dot_general(x[n].astype(BF16), inv[src, within], NT, preferred_element_type=F32)
                lf[n] = f
                solved.append((n, f.astype(BF16)))
        for n, f in solved:
            r = lax.dot_general(f, u[pl.ds(n * PER, PER)].reshape(PER * W, W), NT, preferred_element_type=F32)
            for b in range(PER):
                t[n * PER + b] = r[:, b * W : (b + 1) * W]
        return 0

    lax.fori_loop(0, 8, forward, 0)
    to_smem.wait()
    pl.semaphore_wait(ready.at[1], 2)

    def sum_of(p):
        return (t[idx_s[0, p]] + t[idx_s[1, p]]) + (t[idx_s[2, p]] + t[idx_s[3, p]])

    def at_z(d, yy, cc):
        return ((yy * NZ + (z + d) % NZ) * NC + cc) * 2

    z_order = (4, 3, 5, 2, 6, 1, 7, 0)

    def at_y(d, k, cc):
        return ((((y + d) % NY) * NZ + (z + z_order[k]) % NZ) * NC + cc) * 2 + 1

    def sib_z(d):
        sums = [sum_of(at_z(d, k, 1 - c)).astype(BF16) for k in range(NY)]
        for k in range(NY):
            az[d, k] = sums[k]
        send(az.at[d], bz.at[d], csz, crz.at[d], sibling)

    def sib_y(d):
        for h in range(0, NZ, 4):
            sums = [sum_of(at_y(d, h + k, 1 - c)).astype(BF16) for k in range(4)]
            for k in range(4):
                ay[d, h + k] = sums[k]
        send(ay.at[d], by.at[d], csy, cry.at[d], sibling)

    def has_z(d):
        arrived(bz.at[d], crz.at[d])

    def has_y(d):
        arrived(by.at[d], cry.at[d])

    def sum_z(d, k):
        return sum_of(at_z(d, k, c)) + bz[d, k].astype(F32)

    def sum_y(d, k):
        return sum_of(at_y(d, k, c)) + by[d, k].astype(F32)

    lower, upper = pl.ds(0, 2), pl.ds(2, 2)

    def own_z(d, part, more=()):
        sums = []
        for k in part:
            v = sum_z(d, k)
            for got in more:
                v = v + rz[got, k].astype(F32)
            sums.append(v.astype(BF16))
        for k, v in zip(part, sums):
            oz[d, k] = v

    def along(kind, d, way, to, part, sem):
        here = pl.ds(part[0], len(part))
        send(oz.at[d, here], rz.at[way * 4 + kind, here], zs, sem, off_z(to if way == 0 else NZ - to))

    def wait_z(kind, way, part, sem):
        arrived(rz.at[way * 4 + kind, pl.ds(part[0], len(part))], sem)

    def own_y(d, h):
        sums = [sum_y(d, h + k).astype(BF16) for k in range(4)]
        for k in range(4):
            oy[d, h + k] = sums[k]
        here = pl.ds(h, 4)
        send(oy.at[d, here], ry.at[d, here], ys, yr.at[h // 4], off_y(d))

    lower, upper, every = (0, 1), (2, 3), (0, 1, 2, 3)
    firsts, seconds = (lower, upper), (upper, lower)
    sib_z(4), sib_z(3), sib_z(5), sib_y(2)
    has_z(4)
    own_z(4, every)
    for way in range(2):
        along(1, 4, way, 2, firsts[way], zr.at[way, 0])
    for way, d in ((0, 3), (1, 5)):
        has_z(d)
        own_z(d, every)
        along(0, d, way, 1, firsts[way], zr.at[way, 1])
    for way, d in ((0, 3), (1, 5)):
        along(0, d, way, 1, seconds[way], zr.at[way, 2])
    sib_y(1), sib_y(3), sib_z(1), sib_z(7)
    has_y(2)
    own_y(2, 0)
    has_y(1)
    own_y(1, 0)
    has_y(3)
    own_y(3, 0)
    for d in (2, 1, 3):
        own_y(d, 4)
    for way, d in ((0, 1), (1, 7)):
        has_z(d)
        own_z(d, every)
        along(2, d, way, 1, every, last_z)
    sib_z(2), sib_z(6), sib_y(0), sib_z(0)
    for way, d in ((0, 2), (1, 6)):
        has_z(d)
        wait_z(1, way, firsts[way], zr.at[way, 0])
        wait_z(0, way, firsts[way], zr.at[way, 1])
        own_z(d, firsts[way], (way * 4, way * 4 + 1))
        along(3, d, way, 2, firsts[way], last_z)
    for way, d in ((0, 2), (1, 6)):
        wait_z(0, way, seconds[way], zr.at[way, 2])
        own_z(d, seconds[way], (way * 4,))
        along(3, d, way, 2, seconds[way], last_z)

    has_y(0)
    for h in range(2):
        arrived(ry.at[pl.ds(1, 3), pl.ds(4 * h, 4)], yr.at[h])
        for k in range(4 * h, 4 * h + 4):
            d = z_order[k]
            v = sum_y(0, k) + (ry[1, k].astype(F32) + ry[2, k].astype(F32)) + ry[3, k].astype(F32)
            if d:
                o2[d] = v.astype(BF16)
                send(o2.at[d], r2.at[d], s2, q2, off_z(d))
            else:
                keep[...] = v
    has_z(0)
    arrived(rz.at[pl.ds(0, 4)], last_z)
    for k in range(NY):
        v = sum_z(0, k) + (rz[2, k].astype(F32) + rz[3, k].astype(F32)) + (rz[6, k].astype(F32) + rz[7, k].astype(F32))
        r3[y, k] = v.astype(BF16)
    for d in (2, 1, 3):
        send(r3.at[y], r3.at[y], s3, q3, off_y(d))

    def blk(j, zz, yy, n=1):
        return g.at[pl.ds((c * 2 + j) * (UPPER // 4) + ((zz + NZ) % NZ) * NY + (yy + NY) % NY, n)]

    def solve(right, total, factor):
        v = (right - total).astype(BF16)
        h = lax.dot_general(v, factor, NT, preferred_element_type=F32).astype(BF16)
        return lax.dot_general(h, factor, NN, preferred_element_type=F32)

    def out1(d):
        b = blk(1, z - d, y)
        for dy in (2, 1, 3):
            send(b, b, gs, ayr.at[d], off_y(dy))
        send(b, b, gs, br, sibling)

    total = keep[...]
    arrived(r2.at[pl.ds(1, NZ - 1)], q2)
    for d in range(1, NZ):
        total = total + r2[d].astype(F32)
    v = solve(ur1[...], total, ui1[...])
    us[1] = v
    g[(c * 2 + 1) * (UPPER // 4) + z * NY + y] = v.astype(BF16)
    b = blk(1, z, y)
    for d in (4, 3, 5, 2, 6, 1, 7):
        send(b, b, gs, azr.at[d], off_z(d))
    out1(0)

    arrived(ui.at[pl.ds(0, NY - 1)], mr.at[0])
    arrived(ur.at[pl.ds(0, NY - 1)], mr.at[1])
    arrived(r3.at[pl.ds(0, NY - 1)], q3)
    for k in range(NY):
        total = (r3[0, k].astype(F32) + r3[1, k].astype(F32)) + (r3[2, k].astype(F32) + r3[3, k].astype(F32))
        v = solve(ur[k], total, ui[k])
        solved_y[k] = v
        g[c * 2 * (UPPER // 4) + z * NY + k] = v.astype(BF16)
    us[0] = solved_y[y]

    def in1(d):
        arrived(blk(1, z - d, y), azr.at[d])
        out1(d)

    def along_y(d):
        arrived(g.at[pl.ds(0, NY - 1)], ayr.at[d])
        for dy in (1, 3, 2):
            b = blk(1, z - d, y - dy)
            send(b, b, gs, br, sibling)

    def ring_piece(way, k, mine=0):
        s, first = ((1, 0), (2, 1), (2, 0), (3, 1), (3, 0), (4, 1))[k]
        s = s - mine
        zz = z - s if way == 0 else z + s
        return (zz, 0, NY) if k == 0 else (zz, 2 * (1 - first if way == 0 else first), 2)

    def hop(way, n):
        return off_z(n if way == 0 else NZ - n)

    def along_z(k):
        for way in range(2):
            b = blk(0, *ring_piece(way, k))
            arrived(b, arr.at[way, k])
            if k in (1, 2):
                send(b, b, gs, arr.at[way, k + 2], hop(way, 1))
            if k == 1:
                send(b, b, gs, arr.at[way, 5], hop(way, 2))
            send(b, b, gs, br, sibling)

    for k in (1, 2, 0):
        for way in range(2):
            b = blk(0, *ring_piece(way, k, 2 if k else 1))
            send(b, b, gs, arr.at[way, k], hop(way, 2 if k else 1))
    b = blk(0, z, 0, NY)
    send(b, b, gs, br, sibling)
    in1(1), in1(7), in1(2), in1(6), along_y(0), in1(3), in1(5), in1(4)
    along_y(1), along_y(7), along_z(1), along_z(2), along_y(2), along_y(6)
    along_y(3), along_y(5), along_z(0), along_y(4), along_z(3), along_z(4), along_z(5)
    arrived(g.at[pl.ds(0, UPPER // 2)], br)

    def backward(i, _):
        backs = []
        for q in range(8):
            n = i * 8 + q
            parts = []
            for b in range(PER):
                k = n * PER + b
                parts.append(g[idx_s[CAP + k // W, k % W]])
            corr = lax.dot_general(
                jnp.concatenate(parts, axis=1), u[pl.ds(n * PER, PER)].reshape(PER * W, W), NN, preferred_element_type=F32
            )
            backs.append((lf[n] - corr).astype(BF16))
        for q in range(8):
            lo[i * 8 + q] = lax.dot_general(backs[q], inv[i, q], NN, preferred_element_type=F32)
        return 0

    lax.fori_loop(0, 4, backward, 0)
    sent(pk.at[pl.ds(0, 3)], xs)
    sent(az, csz)
    sent(ay, csy)
    sent(oz.at[pl.ds(0, 7)], zs)
    sent(oy.at[pl.ds(0, 3)], ys)
    sent(o2.at[pl.ds(0, NZ - 1)], s2)
    sent(r3.at[pl.ds(0, NY - 1)], s3)
    sent(g.at[pl.ds(0, 123)], gs)
    sent(ui.at[pl.ds(0, NY - 1)], ms.at[0])
    sent(ur.at[pl.ds(0, NY - 1)], ms.at[1])


def on_device(leaf_right, upper_right, leaf_inverse, upper_inverse, update_blocks, block_target, upper_place):
    hbm = pl.BlockSpec(memory_space=pltpu.HBM)
    vmem = pl.BlockSpec(memory_space=pltpu.VMEM)
    dma = pltpu.SemaphoreType.DMA
    leaves = NX * GROUP
    half = lambda *shape: pltpu.VMEM(shape + (COLS, W), BF16)
    wide = lambda *shape: pltpu.VMEM(shape + (COLS, W), F32)
    return pl.pallas_call(
        kernel,
        out_shape=(pltpu.VMEM((leaves, COLS, W), F32), pltpu.VMEM((2, COLS, W), F32)),
        in_specs=[hbm] * 7,
        out_specs=(vmem, vmem),
        scratch_shapes=[
            pltpu.VMEM((1, BLOCKS), I32),
            pltpu.VMEM((1, W), I32),
            pltpu.VMEM((BLOCKS, W, W), BF16),
            wide(leaves),
            pltpu.VMEM((NX, 2, 2, 9, STRIP, W), BF16),
            pltpu.VMEM((NX, GROUP, W, W), BF16),
            wide(leaves),
            wide(BLOCKS + 1),
            pltpu.VMEM((8, W), I32),
            pltpu.SMEM((8, W), I32),
            half(NZ, NY), half(NY, NZ),
            half(NZ, NY), half(NY, NZ),
            half(NZ, NY), half(NY, NZ),
            half(8, NY), half(NY, NZ),
            half(NZ), half(NZ),
            half(NY, NY),
            wide(),
            wide(NY),
            pltpu.VMEM((NY, W, W), BF16),
            wide(),
            pltpu.VMEM((W, W), BF16),
            wide(NY),
            half(UPPER),
            dma((17,)),
            dma((6, 2)),
            dma((NZ,)), dma((NY,)),
            dma((2, 3)), dma, dma((2,)),
            dma, dma,
            dma((NZ,)), dma((NZ,)), dma((2, 6)), dma, dma((2,)),
            dma, dma, dma, dma, dma, dma, dma, dma,
            dma((2,)),
            pltpu.SemaphoreType.REGULAR((3,)),
        ],
        compiler_params=pltpu.CompilerParams(
            collective_id=0, has_side_effects=True, vmem_limit_bytes=59 * 2**20
        ),
        name="solve",
    )(block_target.reshape(1, -1), upper_place.reshape(1, -1), leaf_right, upper_right, leaf_inverse, upper_inverse, update_blocks)


def solution(mesh):
    return jax.shard_map(
        on_device,
        mesh=mesh,
        in_specs=(
            P("leaf", "rhs", None),
            P("leaf", "rhs", None),
            P(("leaf", "rhs"), None, None),
            P("leaf", None, None),
            P("leaf", None, None),
            P("leaf", None),
            P(),
        ),
        out_specs=(P("leaf", "rhs", None), P("leaf", "rhs", None)),
        check_vma=False,
    )
```

```python
import jax
import jax.numpy as jnp
from jax import lax
from jax.experimental import pallas as pl
from jax.experimental.pallas import tpu as pltpu
from jax.sharding import PartitionSpec as P

MESH = pl.DeviceIdType.MESH
F32, BF16, I32 = jnp.float32, jnp.bfloat16, jnp.int32
NX, NY, NZ, NC = 4, 4, 8, 2
PER = 8
GROUP = 8
COLS, W = 64, 128
BLOCKS = 256
CAP = 4
UPPER = NY * NZ * NC * 2
STRIP = 16
NT = (((1,), (1,)), ((), ()))
NN = (((1,), (0,)), ((), ()))


def kernel(
    target_hbm, place_hbm, right_hbm, upper_right_hbm, inv_hbm, upper_inv_hbm, u_hbm,
    lo, us,
    target_ref, place_ref, u, x, pk, inv, lf, t, idx_v, idx_s, az, ay, bz, by, oz, oy, rz, ry,
    o2, r2, r3, keep, ur, ui, ur1, ui1, solved_y, g,
    loc, xr, crz, cry, zr, last_z, yr, q2, q3, azr, ayr, arr, br, mr,
    xs, csz, csy, zs, ys, s2, s3, gs, ms, ready,
):
    leaf, rx = lax.axis_index("leaf"), lax.axis_index("rhs")
    y, z, c = leaf // (NZ * NC), (leaf // NC) % NZ, leaf % NC

    def at(yy, zz, cc, xx):
        return ((yy * NZ + zz) * NC + cc, xx)

    def off_x(d):
        return at(y, z, c, (rx + d) % NX)

    def off_y(d):
        return at((y + d) % NY, z, c, rx)

    def off_z(d):
        return at(y, (z + d) % NZ, c, rx)

    sibling = at(y, z, 1 - c, rx)

    def remote(src, dst, ssem, rsem, dev):
        return pltpu.make_async_remote_copy(
            src_ref=src, dst_ref=dst, send_sem=ssem, recv_sem=rsem, device_id=dev, device_id_type=MESH
        )

    def send(src, dst, ssem, rsem, dev):
        remote(src, dst, ssem, rsem, dev).start()

    def arrived(ref, rsem):
        remote(ref, ref, xs, rsem, sibling).wait_recv()

    def sent(ref, ssem):
        remote(ref, ref, ssem, br, sibling).wait_send()

    barrier = pltpu.get_barrier_semaphore()
    peers = [off_x(1), off_x(3)] + [off_y(1), off_y(3), off_z(1), off_z(7), sibling]
    for dev in peers:
        pl.semaphore_signal(barrier, inc=1, device_id=dev, device_id_type=MESH)

    own = pltpu.make_async_copy(inv_hbm, inv.at[rx], loc.at[0])
    own.start()
    load_target = pltpu.make_async_copy(target_hbm, target_ref, loc.at[5])
    load_target.start()
    load_place = pltpu.make_async_copy(place_hbm, place_ref, loc.at[6])
    load_place.start()

    def pair_of(i, m):
        d = jnp.where(i < 2, 0, jnp.where(i >= 6, 2, 1 + 2 * (i % 2)))
        half = jnp.where(i >= 6, m, jnp.where((i == 4) | (i == 5), 1 - i % 2, i % 2))
        return (rx + NX - d) % NX, half, jnp.where(i >= 6, i % 2, m)

    def load_u(i, m):
        src, half, q = pair_of(i, m)
        part = pl.ds((src * 4 + half * 2 + q) * (2 * PER), 2 * PER)
        return pltpu.make_async_copy(u_hbm.at[part], u.at[part], loc.at[7 + i])

    load_x = pltpu.make_async_copy(right_hbm, x, loc.at[1])
    load_x.start()

    def start_u(i, _):
        load_u(i, 0).start()
        load_u(i, 1).start()
        return 0

    lax.fori_loop(0, 8, start_u, 0)
    uppers = [
        pltpu.make_async_copy(upper_right_hbm.at[0], ur.at[y], loc.at[2]),
        pltpu.make_async_copy(upper_right_hbm.at[1], ur1, loc.at[3]),
        pltpu.make_async_copy(upper_inv_hbm.at[0], ui.at[y], loc.at[15]),
        pltpu.make_async_copy(upper_inv_hbm.at[1], ui1, loc.at[16]),
    ]
    for cp in uppers:
        cp.start()

    own.wait()
    lane16 = lax.broadcasted_iota(I32, (STRIP, W), 1)

    def strip(n, s):
        return inv[rx, n, s * STRIP : (s + 1) * STRIP, :].astype(F32)

    for h in range(2):
        for q in range(2):
            two = (h * 4 + q * 2, h * 4 + q * 2 + 1)
            for m, n in enumerate(two):
                for s in range(3):
                    pk[rx, h, q, m * 3 + s] = (strip(n, 6 - s) + pltpu.roll(strip(n, s), STRIP * (7 - s), 1)).astype(BF16)
                pk[rx, h, q, 6 + m] = inv[rx, n, 7 * STRIP :, :]
            pk[rx, h, q, 8] = (strip(two[0], 3) + pltpu.roll(strip(two[1], 3), W // 2, 1)).astype(BF16)

    pl.semaphore_wait(barrier, len(peers))

    def pass_on(i, near):
        for d in (near, NZ - near):
            pl.semaphore_signal(ready.at[i], inc=1, device_id=off_z(d), device_id_type=MESH)

    pass_on(0, 1)
    for d in (1, NY - 1):
        pl.semaphore_signal(ready.at[2], inc=1, device_id=off_y(d), device_id_type=MESH)

    for h, i, d in ((0, 2, 1), (1, 3, 3), (1, 4, 1), (0, 5, 3)):
        for q in range(2):
            b = pk.at[rx, h, q]
            send(b, b, xs, xr.at[i - 2, q], off_x(d))
    relays = []
    for h, d in ((0, 1), (1, 3)):
        for q in range(2):
            b = pk.at[(rx + NX - d) % NX, h, q]
            relays.append(remote(b, b, xs, xr.at[4 + q, h], off_x(d)))
    load_target.wait()
    load_place.wait()
    lane = lax.broadcasted_iota(I32, (BLOCKS, W), 1)
    row = lax.broadcasted_iota(I32, (BLOCKS, W), 0)
    target = jnp.concatenate(
        [
            jnp.sum(jnp.where(lane[:W] == row[:W], target_ref[:, h * W : (h + 1) * W], 0), axis=1, keepdims=True)
            for h in range(BLOCKS // W)
        ],
        axis=0,
    )
    pos = jnp.sum(jnp.where(target == lane, place_ref[...], 0), axis=1, keepdims=True)
    cand = jnp.where(pos == lane, row, BLOCKS)
    for s in range(CAP):
        low = jnp.min(cand, axis=0, keepdims=True)
        idx_v[s : s + 1, :] = low
        cand = jnp.where(cand > low, cand, BLOCKS)
    where_in_g = (((pos // 2) % 2) * 2 + pos % 2) * (UPPER // 4) + ((pos // 4) % NZ) * NY + pos // (4 * NZ)
    for h in range(BLOCKS // W):
        idx_v[CAP + h : CAP + h + 1, :] = jnp.sum(jnp.where(row - h * W == lane, where_in_g, 0), axis=0, keepdims=True)
    idx_v[CAP + 2 :, :] = jnp.zeros((8 - CAP - 2, W), I32)
    to_smem = pltpu.make_async_copy(idx_v, idx_s, loc.at[4])
    to_smem.start()

    t[BLOCKS] = jnp.zeros((COLS, W), F32)
    load_x.wait()

    def forward(i, _):
        @pl.when(i == 2)
        def _():
            pl.semaphore_wait(ready.at[0], 2)
            pass_on(1, 2)

        @pl.when(i == 4)
        def _():
            for cp in uppers:
                cp.wait()
            pl.semaphore_wait(ready.at[2], 2)
            for d in (2, 1, 3):
                send(ui.at[y], ui.at[y], ms.at[0], mr.at[0], off_y(d))
                send(ur.at[y], ur.at[y], ms.at[1], mr.at[1], off_y(d))

        @pl.when(i >= 2)
        def _():
            for m in range(2):
                src, half, q = pair_of(i, m)
                arrived(pk.at[src, half, q], xr.at[i - 2, m])
                for h in range(2):

                    @pl.when(i == 2 + h)
                    def _():
                        relays[2 * h + m].start()

            for m in range(2):
                src, half, q = pair_of(i, m)
                for e in range(2):
                    n = half * 4 + q * 2 + e
                    for s in range(3):
                        both = pk[src, half, q, e * 3 + s].astype(F32)
                        cut = STRIP * (7 - s)
                        inv[src, n, (6 - s) * STRIP : (7 - s) * STRIP, :] = jnp.where(lane16 < cut, both, 0.0).astype(BF16)
                        inv[src, n, s * STRIP : (s + 1) * STRIP, :] = jnp.where(
                            lane16 < W - cut, pltpu.roll(both, W - cut, 1), 0.0
                        ).astype(BF16)
                    inv[src, n, 7 * STRIP :, :] = pk[src, half, q, 6 + e]
                    both = pk[src, half, q, 8].astype(F32)
                    if e:
                        both = pltpu.roll(both, W // 2, 1)
                    inv[src, n, 3 * STRIP : 4 * STRIP, :] = jnp.where(lane16 < W // 2, both, 0.0).astype(BF16)

        some = u.at[pl.ds(0, 4 * PER)]
        pltpu.make_async_copy(some, some, loc.at[7 + i]).wait()
        solved = []
        for m in range(2):
            src, half, q = pair_of(i, m)
            for e in range(2):
                within = half * 4 + q * 2 + e
                n = src * GROUP + within
                f = lax.dot_general(x[n].astype(BF16), inv[src, within], NT, preferred_element_type=F32)
                lf[n] = f
                solved.append((n, f.astype(BF16)))
        for n, f in solved:
            r = lax.dot_general(f, u[pl.ds(n * PER, PER)].reshape(PER * W, W), NT, preferred_element_type=F32)
            for b in range(PER):
                t[n * PER + b] = r[:, b * W : (b + 1) * W]
        return 0

    lax.fori_loop(0, 8, forward, 0)
    to_smem.wait()
    pl.semaphore_wait(ready.at[1], 2)

    def sum_of(p):
        return (t[idx_s[0, p]] + t[idx_s[1, p]]) + (t[idx_s[2, p]] + t[idx_s[3, p]])

    def at_z(d, yy, cc):
        return ((yy * NZ + (z + d) % NZ) * NC + cc) * 2

    z_order = (4, 3, 5, 2, 6, 1, 7, 0)

    def at_y(d, k, cc):
        return ((((y + d) % NY) * NZ + (z + z_order[k]) % NZ) * NC + cc) * 2 + 1

    def sib_z(d):
        sums = [sum_of(at_z(d, k, 1 - c)).astype(BF16) for k in range(NY)]
        for k in range(NY):
            az[d, k] = sums[k]
        send(az.at[d], bz.at[d], csz, crz.at[d], sibling)

    def sib_y(d):
        for h in range(0, NZ, 4):
            sums = [sum_of(at_y(d, h + k, 1 - c)).astype(BF16) for k in range(4)]
            for k in range(4):
                ay[d, h + k] = sums[k]
        send(ay.at[d], by.at[d], csy, cry.at[d], sibling)

    def has_z(d):
        arrived(bz.at[d], crz.at[d])

    def has_y(d):
        arrived(by.at[d], cry.at[d])

    def sum_z(d, k):
        return sum_of(at_z(d, k, c)) + bz[d, k].astype(F32)

    def sum_y(d, k):
        return sum_of(at_y(d, k, c)) + by[d, k].astype(F32)

    lower, upper = pl.ds(0, 2), pl.ds(2, 2)

    def own_z(d, part, more=()):
        sums = []
        for k in part:
            v = sum_z(d, k)
            for got in more:
                v = v + rz[got, k].astype(F32)
            sums.append(v.astype(BF16))
        for k, v in zip(part, sums):
            oz[d, k] = v

    def along(kind, d, way, to, part, sem):
        here = pl.ds(part[0], len(part))
        send(oz.at[d, here], rz.at[way * 4 + kind, here], zs, sem, off_z(to if way == 0 else NZ - to))

    def wait_z(kind, way, part, sem):
        arrived(rz.at[way * 4 + kind, pl.ds(part[0], len(part))], sem)

    def own_y(d, h):
        sums = [sum_y(d, h + k).astype(BF16) for k in range(4)]
        for k in range(4):
            oy[d, h + k] = sums[k]
        here = pl.ds(h, 4)
        send(oy.at[d, here], ry.at[d, here], ys, yr.at[h // 4], off_y(d))

    lower, upper, every = (0, 1), (2, 3), (0, 1, 2, 3)
    firsts, seconds = (lower, upper), (upper, lower)
    sib_z(4), sib_z(3), sib_z(5), sib_y(2)
    has_z(4)
    own_z(4, every)
    for way in range(2):
        along(1, 4, way, 2, firsts[way], zr.at[way, 0])
    for way, d in ((0, 3), (1, 5)):
        has_z(d)
        own_z(d, every)
        along(0, d, way, 1, firsts[way], zr.at[way, 1])
    for way, d in ((0, 3), (1, 5)):
        along(0, d, way, 1, seconds[way], zr.at[way, 2])
    sib_y(1), sib_y(3), sib_z(1), sib_z(7)
    has_y(2)
    own_y(2, 0)
    has_y(1)
    own_y(1, 0)
    has_y(3)
    own_y(3, 0)
    for d in (2, 1, 3):
        own_y(d, 4)
    for way, d in ((0, 1), (1, 7)):
        has_z(d)
        own_z(d, every)
        along(2, d, way, 1, every, last_z)
    sib_z(2), sib_z(6), sib_y(0), sib_z(0)
    for way, d in ((0, 2), (1, 6)):
        has_z(d)
        wait_z(1, way, firsts[way], zr.at[way, 0])
        wait_z(0, way, firsts[way], zr.at[way, 1])
        own_z(d, firsts[way], (way * 4, way * 4 + 1))
        along(3, d, way, 2, firsts[way], last_z)
    for way, d in ((0, 2), (1, 6)):
        wait_z(0, way, seconds[way], zr.at[way, 2])
        own_z(d, seconds[way], (way * 4,))
        along(3, d, way, 2, seconds[way], last_z)

    has_y(0)
    for h in range(2):
        arrived(ry.at[pl.ds(1, 3), pl.ds(4 * h, 4)], yr.at[h])
        for k in range(4 * h, 4 * h + 4):
            d = z_order[k]
            v = sum_y(0, k) + (ry[1, k].astype(F32) + ry[2, k].astype(F32)) + ry[3, k].astype(F32)
            if d:
                o2[d] = v.astype(BF16)
                send(o2.at[d], r2.at[d], s2, q2, off_z(d))
            else:
                keep[...] = v
    has_z(0)
    arrived(rz.at[pl.ds(0, 4)], last_z)
    for k in range(NY):
        v = sum_z(0, k) + (rz[2, k].astype(F32) + rz[3, k].astype(F32)) + (rz[6, k].astype(F32) + rz[7, k].astype(F32))
        r3[y, k] = v.astype(BF16)
    for d in (2, 1, 3):
        send(r3.at[y], r3.at[y], s3, q3, off_y(d))

    def blk(j, zz, yy, n=1):
        return g.at[pl.ds((c * 2 + j) * (UPPER // 4) + ((zz + NZ) % NZ) * NY + (yy + NY) % NY, n)]

    def solve(right, total, factor):
        v = (right - total).astype(BF16)
        h = lax.dot_general(v, factor, NT, preferred_element_type=F32).astype(BF16)
        return lax.dot_general(h, factor, NN, preferred_element_type=F32)

    def out1(d):
        b = blk(1, z - d, y)
        for dy in (2, 1, 3):
            send(b, b, gs, ayr.at[d], off_y(dy))
        send(b, b, gs, br, sibling)

    total = keep[...]
    arrived(r2.at[pl.ds(1, NZ - 1)], q2)
    for d in range(1, NZ):
        total = total + r2[d].astype(F32)
    v = solve(ur1[...], total, ui1[...])
    us[1] = v
    g[(c * 2 + 1) * (UPPER // 4) + z * NY + y] = v.astype(BF16)
    b = blk(1, z, y)
    for d in (4, 3, 5, 2, 6, 1, 7):
        send(b, b, gs, azr.at[d], off_z(d))
    out1(0)

    arrived(ui.at[pl.ds(0, NY - 1)], mr.at[0])
    arrived(ur.at[pl.ds(0, NY - 1)], mr.at[1])
    arrived(r3.at[pl.ds(0, NY - 1)], q3)
    for k in range(NY):
        total = (r3[0, k].astype(F32) + r3[1, k].astype(F32)) + (r3[2, k].astype(F32) + r3[3, k].astype(F32))
        v = solve(ur[k], total, ui[k])
        solved_y[k] = v
        g[c * 2 * (UPPER // 4) + z * NY + k] = v.astype(BF16)
    us[0] = solved_y[y]

    def in1(d):
        arrived(blk(1, z - d, y), azr.at[d])
        out1(d)

    def along_y(d):
        arrived(g.at[pl.ds(0, NY - 1)], ayr.at[d])
        for dy in (1, 3, 2):
            b = blk(1, z - d, y - dy)
            send(b, b, gs, br, sibling)

    def ring_piece(way, k, mine=0):
        s, first = ((1, 0), (2, 1), (2, 0), (3, 1), (3, 0), (4, 1))[k]
        s = s - mine
        zz = z - s if way == 0 else z + s
        return (zz, 0, NY) if k == 0 else (zz, 2 * (1 - first if way == 0 else first), 2)

    def hop(way, n):
        return off_z(n if way == 0 else NZ - n)

    def along_z(k):
        for way in range(2):
            b = blk(0, *ring_piece(way, k))
            arrived(b, arr.at[way, k])
            if k in (1, 2):
                send(b, b, gs, arr.at[way, k + 2], hop(way, 1))
            if k == 1:
                send(b, b, gs, arr.at[way, 5], hop(way, 2))
            send(b, b, gs, br, sibling)

    for k in (1, 2, 0):
        for way in range(2):
            b = blk(0, *ring_piece(way, k, 2 if k else 1))
            send(b, b, gs, arr.at[way, k], hop(way, 2 if k else 1))
    b = blk(0, z, 0, NY)
    send(b, b, gs, br, sibling)
    in1(1), in1(7), in1(2), in1(6), in1(3), in1(5), along_y(0), in1(4)
    along_z(1), along_y(1), along_y(7), along_z(2), along_y(2), along_y(6)
    along_z(0), along_y(3), along_y(5), along_z(3), along_z(5), along_y(4), along_z(4)
    arrived(g.at[pl.ds(0, UPPER // 2)], br)

    def backward(i, _):
        backs = []
        for q in range(16):
            n = i * 16 + q
            parts = []
            for b in range(PER):
                k = n * PER + b
                parts.append(g[idx_s[CAP + k // W, k % W]])
            corr = lax.dot_general(
                jnp.concatenate(parts, axis=1), u[pl.ds(n * PER, PER)].reshape(PER * W, W), NN, preferred_element_type=F32
            )
            backs.append((lf[n] - corr).astype(BF16))
        for q in range(16):
            lo[i * 16 + q] = lax.dot_general(backs[q], inv[i * 2 + q // 8, q % 8], NN, preferred_element_type=F32)
        return 0

    lax.fori_loop(0, 2, backward, 0)
    sent(pk.at[pl.ds(0, 3)], xs)
    sent(az, csz)
    sent(ay, csy)
    sent(oz.at[pl.ds(0, 7)], zs)
    sent(oy.at[pl.ds(0, 3)], ys)
    sent(o2.at[pl.ds(0, NZ - 1)], s2)
    sent(r3.at[pl.ds(0, NY - 1)], s3)
    sent(g.at[pl.ds(0, 123)], gs)
    sent(ui.at[pl.ds(0, NY - 1)], ms.at[0])
    sent(ur.at[pl.ds(0, NY - 1)], ms.at[1])


def on_device(leaf_right, upper_right, leaf_inverse, upper_inverse, update_blocks, block_target, upper_place):
    hbm = pl.BlockSpec(memory_space=pltpu.HBM)
    vmem = pl.BlockSpec(memory_space=pltpu.VMEM)
    dma = pltpu.SemaphoreType.DMA
    leaves = NX * GROUP
    half = lambda *shape: pltpu.VMEM(shape + (COLS, W), BF16)
    wide = lambda *shape: pltpu.VMEM(shape + (COLS, W), F32)
    return pl.pallas_call(
        kernel,
        out_shape=(pltpu.VMEM((leaves, COLS, W), F32), pltpu.VMEM((2, COLS, W), F32)),
        in_specs=[hbm] * 7,
        out_specs=(vmem, vmem),
        scratch_shapes=[
            pltpu.VMEM((1, BLOCKS), I32),
            pltpu.VMEM((1, W), I32),
            pltpu.VMEM((BLOCKS, W, W), BF16),
            wide(leaves),
            pltpu.VMEM((NX, 2, 2, 9, STRIP, W), BF16),
            pltpu.VMEM((NX, GROUP, W, W), BF16),
            wide(leaves),
            wide(BLOCKS + 1),
            pltpu.VMEM((8, W), I32),
            pltpu.SMEM((8, W), I32),
            half(NZ, NY), half(NY, NZ),
            half(NZ, NY), half(NY, NZ),
            half(NZ, NY), half(NY, NZ),
            half(8, NY), half(NY, NZ),
            half(NZ), half(NZ),
            half(NY, NY),
            wide(),
            wide(NY),
            pltpu.VMEM((NY, W, W), BF16),
            wide(),
            pltpu.VMEM((W, W), BF16),
            wide(NY),
            half(UPPER),
            dma((17,)),
            dma((6, 2)),
            dma((NZ,)), dma((NY,)),
            dma((2, 3)), dma, dma((2,)),
            dma, dma,
            dma((NZ,)), dma((NZ,)), dma((2, 6)), dma, dma((2,)),
            dma, dma, dma, dma, dma, dma, dma, dma,
            dma((2,)),
            pltpu.SemaphoreType.REGULAR((3,)),
        ],
        compiler_params=pltpu.CompilerParams(
            collective_id=0, has_side_effects=True, vmem_limit_bytes=59 * 2**20
        ),
        name="solve",
    )(block_target.reshape(1, -1), upper_place.reshape(1, -1), leaf_right, upper_right, leaf_inverse, upper_inverse, update_blocks)


def solution(mesh):
    return jax.shard_map(
        on_device,
        mesh=mesh,
        in_specs=(
            P("leaf", "rhs", None),
            P("leaf", "rhs", None),
            P(("leaf", "rhs"), None, None),
            P("leaf", None, None),
            P("leaf", None, None),
            P("leaf", None),
            P(),
        ),
        out_specs=(P("leaf", "rhs", None), P("leaf", "rhs", None)),
        check_vma=False,
    )
```

```python
import jax
import jax.numpy as jnp
from jax import lax
from jax.experimental import pallas as pl
from jax.experimental.pallas import tpu as pltpu
from jax.sharding import PartitionSpec as P

MESH = pl.DeviceIdType.MESH
F32, BF16, I32 = jnp.float32, jnp.bfloat16, jnp.int32
NX, NY, NZ, NC = 4, 4, 8, 2
PER = 8
GROUP = 8
COLS, W = 64, 128
BLOCKS = 256
CAP = 4
UPPER = NY * NZ * NC * 2
STRIP = 16
NT = (((1,), (1,)), ((), ()))
NN = (((1,), (0,)), ((), ()))


def kernel(
    target_hbm, place_hbm, right_hbm, upper_right_hbm, inv_hbm, upper_inv_hbm, u_hbm,
    lo, us,
    target_ref, place_ref, u, x, pk, inv, lf, t, idx_v, idx_s, az, ay, bz, by, oz, oy, rz, ry,
    o2, r2, r3, keep, ur, ui, ur1, ui1, solved_y, g,
    loc, xr, crz, cry, zr, last_z, yr, q2, q3, azr, ayr, arr, br, mr,
    xs, csz, csy, zs, ys, s2, s3, gs, ms, ready,
):
    leaf, rx = lax.axis_index("leaf"), lax.axis_index("rhs")
    y, z, c = leaf // (NZ * NC), (leaf // NC) % NZ, leaf % NC

    def at(yy, zz, cc, xx):
        return ((yy * NZ + zz) * NC + cc, xx)

    def off_x(d):
        return at(y, z, c, (rx + d) % NX)

    def off_y(d):
        return at((y + d) % NY, z, c, rx)

    def off_z(d):
        return at(y, (z + d) % NZ, c, rx)

    sibling = at(y, z, 1 - c, rx)

    def remote(src, dst, ssem, rsem, dev):
        return pltpu.make_async_remote_copy(
            src_ref=src, dst_ref=dst, send_sem=ssem, recv_sem=rsem, device_id=dev, device_id_type=MESH
        )

    def send(src, dst, ssem, rsem, dev):
        remote(src, dst, ssem, rsem, dev).start()

    def arrived(ref, rsem):
        remote(ref, ref, xs, rsem, sibling).wait_recv()

    def sent(ref, ssem):
        remote(ref, ref, ssem, br, sibling).wait_send()

    barrier = pltpu.get_barrier_semaphore()
    peers = [off_x(1), off_x(3)] + [off_y(1), off_y(3), off_z(1), off_z(7), sibling]
    for dev in peers:
        pl.semaphore_signal(barrier, inc=1, device_id=dev, device_id_type=MESH)

    own = pltpu.make_async_copy(inv_hbm, inv.at[rx], loc.at[0])
    own.start()
    load_target = pltpu.make_async_copy(target_hbm, target_ref, loc.at[5])
    load_target.start()
    load_place = pltpu.make_async_copy(place_hbm, place_ref, loc.at[6])
    load_place.start()

    def pair_of(i, m):
        d = jnp.where(i < 2, 0, jnp.where(i >= 6, 2, 1 + 2 * (i % 2)))
        half = jnp.where(i >= 6, m, jnp.where((i == 4) | (i == 5), 1 - i % 2, i % 2))
        return (rx + NX - d) % NX, half, jnp.where(i >= 6, i % 2, m)

    def load_u(i, m):
        src, half, q = pair_of(i, m)
        part = pl.ds((src * 4 + half * 2 + q) * (2 * PER), 2 * PER)
        return pltpu.make_async_copy(u_hbm.at[part], u.at[part], loc.at[7 + i])

    load_x = pltpu.make_async_copy(right_hbm, x, loc.at[1])
    load_x.start()

    def start_u(i, _):
        load_u(i, 0).start()
        load_u(i, 1).start()
        return 0

    lax.fori_loop(0, 8, start_u, 0)
    uppers = [
        pltpu.make_async_copy(upper_right_hbm.at[0], ur.at[y], loc.at[2]),
        pltpu.make_async_copy(upper_right_hbm.at[1], ur1, loc.at[3]),
        pltpu.make_async_copy(upper_inv_hbm.at[0], ui.at[y], loc.at[15]),
        pltpu.make_async_copy(upper_inv_hbm.at[1], ui1, loc.at[16]),
    ]
    for cp in uppers:
        cp.start()

    own.wait()
    lane16 = lax.broadcasted_iota(I32, (STRIP, W), 1)

    def strip(n, s):
        return inv[rx, n, s * STRIP : (s + 1) * STRIP, :].astype(F32)

    for h in range(2):
        for q in range(2):
            two = (h * 4 + q * 2, h * 4 + q * 2 + 1)
            for m, n in enumerate(two):
                for s in range(3):
                    pk[rx, h, q, m * 3 + s] = (strip(n, 6 - s) + pltpu.roll(strip(n, s), STRIP * (7 - s), 1)).astype(BF16)
                pk[rx, h, q, 6 + m] = inv[rx, n, 7 * STRIP :, :]
            pk[rx, h, q, 8] = (strip(two[0], 3) + pltpu.roll(strip(two[1], 3), W // 2, 1)).astype(BF16)

    pl.semaphore_wait(barrier, len(peers))

    def pass_on(i, near):
        for d in (near, NZ - near):
            pl.semaphore_signal(ready.at[i], inc=1, device_id=off_z(d), device_id_type=MESH)

    pass_on(0, 1)
    for d in (1, NY - 1):
        pl.semaphore_signal(ready.at[2], inc=1, device_id=off_y(d), device_id_type=MESH)

    for h, i, d in ((0, 2, 1), (1, 3, 3), (1, 4, 1), (0, 5, 3)):
        for q in range(2):
            b = pk.at[rx, h, q]
            send(b, b, xs, xr.at[i - 2, q], off_x(d))
    relays = []
    for h, d in ((0, 1), (1, 3)):
        for q in range(2):
            b = pk.at[(rx + NX - d) % NX, h, q]
            relays.append(remote(b, b, xs, xr.at[4 + q, h], off_x(d)))
    load_target.wait()
    load_place.wait()
    lane = lax.broadcasted_iota(I32, (BLOCKS, W), 1)
    row = lax.broadcasted_iota(I32, (BLOCKS, W), 0)
    target = jnp.concatenate(
        [
            jnp.sum(jnp.where(lane[:W] == row[:W], target_ref[:, h * W : (h + 1) * W], 0), axis=1, keepdims=True)
            for h in range(BLOCKS // W)
        ],
        axis=0,
    )
    pos = jnp.sum(jnp.where(target == lane, place_ref[...], 0), axis=1, keepdims=True)
    cand = jnp.where(pos == lane, row, BLOCKS)
    for s in range(CAP):
        low = jnp.min(cand, axis=0, keepdims=True)
        idx_v[s : s + 1, :] = low
        cand = jnp.where(cand > low, cand, BLOCKS)
    where_in_g = (((pos // 2) % 2) * 2 + pos % 2) * (UPPER // 4) + ((pos // 4) % NZ) * NY + pos // (4 * NZ)
    for h in range(BLOCKS // W):
        idx_v[CAP + h : CAP + h + 1, :] = jnp.sum(jnp.where(row - h * W == lane, where_in_g, 0), axis=0, keepdims=True)
    idx_v[CAP + 2 :, :] = jnp.zeros((8 - CAP - 2, W), I32)
    to_smem = pltpu.make_async_copy(idx_v, idx_s, loc.at[4])
    to_smem.start()

    t[BLOCKS] = jnp.zeros((COLS, W), F32)
    load_x.wait()

    def forward(i, _):
        @pl.when(i == 2)
        def _():
            pl.semaphore_wait(ready.at[0], 2)
            pass_on(1, 2)

        @pl.when(i == 4)
        def _():
            for cp in uppers:
                cp.wait()
            pl.semaphore_wait(ready.at[2], 2)
            for d in (2, 1, 3):
                send(ui.at[y], ui.at[y], ms.at[0], mr.at[0], off_y(d))
                send(ur.at[y], ur.at[y], ms.at[1], mr.at[1], off_y(d))

        @pl.when(i >= 2)
        def _():
            for m in range(2):
                src, half, q = pair_of(i, m)
                arrived(pk.at[src, half, q], xr.at[i - 2, m])
                for h in range(2):

                    @pl.when(i == 2 + h)
                    def _():
                        relays[2 * h + m].start()

            for m in range(2):
                src, half, q = pair_of(i, m)
                for e in range(2):
                    n = half * 4 + q * 2 + e
                    for s in range(3):
                        both = pk[src, half, q, e * 3 + s].astype(F32)
                        cut = STRIP * (7 - s)
                        inv[src, n, (6 - s) * STRIP : (7 - s) * STRIP, :] = jnp.where(lane16 < cut, both, 0.0).astype(BF16)
                        inv[src, n, s * STRIP : (s + 1) * STRIP, :] = jnp.where(
                            lane16 < W - cut, pltpu.roll(both, W - cut, 1), 0.0
                        ).astype(BF16)
                    inv[src, n, 7 * STRIP :, :] = pk[src, half, q, 6 + e]
                    both = pk[src, half, q, 8].astype(F32)
                    if e:
                        both = pltpu.roll(both, W // 2, 1)
                    inv[src, n, 3 * STRIP : 4 * STRIP, :] = jnp.where(lane16 < W // 2, both, 0.0).astype(BF16)

        some = u.at[pl.ds(0, 4 * PER)]
        pltpu.make_async_copy(some, some, loc.at[7 + i]).wait()
        solved = []
        for m in range(2):
            src, half, q = pair_of(i, m)
            for e in range(2):
                within = half * 4 + q * 2 + e
                n = src * GROUP + within
                f = lax.dot_general(x[n].astype(BF16), inv[src, within], NT, preferred_element_type=F32)
                lf[n] = f
                solved.append((n, f.astype(BF16)))
        for n, f in solved:
            r = lax.dot_general(f, u[pl.ds(n * PER, PER)].reshape(PER * W, W), NT, preferred_element_type=F32)
            for b in range(PER):
                t[n * PER + b] = r[:, b * W : (b + 1) * W]
        return 0

    lax.fori_loop(0, 8, forward, 0)
    to_smem.wait()
    pl.semaphore_wait(ready.at[1], 2)

    def sum_of(p):
        return (t[idx_s[0, p]] + t[idx_s[1, p]]) + (t[idx_s[2, p]] + t[idx_s[3, p]])

    def at_z(d, yy, cc):
        return ((yy * NZ + (z + d) % NZ) * NC + cc) * 2

    z_order = (4, 3, 5, 2, 6, 1, 7, 0)

    def at_y(d, k, cc):
        return ((((y + d) % NY) * NZ + (z + z_order[k]) % NZ) * NC + cc) * 2 + 1

    def sib_z(d):
        sums = [sum_of(at_z(d, k, 1 - c)).astype(BF16) for k in range(NY)]
        for k in range(NY):
            az[d, k] = sums[k]
        send(az.at[d], bz.at[d], csz, crz.at[d], sibling)

    def sib_y(d):
        for h in range(0, NZ, 4):
            sums = [sum_of(at_y(d, h + k, 1 - c)).astype(BF16) for k in range(4)]
            for k in range(4):
                ay[d, h + k] = sums[k]
        send(ay.at[d], by.at[d], csy, cry.at[d], sibling)

    def has_z(d):
        arrived(bz.at[d], crz.at[d])

    def has_y(d):
        arrived(by.at[d], cry.at[d])

    def sum_z(d, k):
        return sum_of(at_z(d, k, c)) + bz[d, k].astype(F32)

    def sum_y(d, k):
        return sum_of(at_y(d, k, c)) + by[d, k].astype(F32)

    lower, upper = pl.ds(0, 2), pl.ds(2, 2)

    def own_z(d, part, more=()):
        sums = []
        for k in part:
            v = sum_z(d, k)
            for got in more:
                v = v + rz[got, k].astype(F32)
            sums.append(v.astype(BF16))
        for k, v in zip(part, sums):
            oz[d, k] = v

    def along(kind, d, way, to, part, sem):
        here = pl.ds(part[0], len(part))
        send(oz.at[d, here], rz.at[way * 4 + kind, here], zs, sem, off_z(to if way == 0 else NZ - to))

    def wait_z(kind, way, part, sem):
        arrived(rz.at[way * 4 + kind, pl.ds(part[0], len(part))], sem)

    def own_y(d, h):
        sums = [sum_y(d, h + k).astype(BF16) for k in range(4)]
        for k in range(4):
            oy[d, h + k] = sums[k]
        here = pl.ds(h, 4)
        send(oy.at[d, here], ry.at[d, here], ys, yr.at[h // 4], off_y(d))

    lower, upper, every = (0, 1), (2, 3), (0, 1, 2, 3)
    firsts, seconds = (lower, upper), (upper, lower)
    sib_y(2), sib_y(1), sib_y(3), sib_z(4), sib_z(3), sib_z(5)
    for d in (2, 1, 3):
        has_y(d)
        own_y(d, 0)
    has_z(4)
    own_z(4, every)
    for way in range(2):
        along(1, 4, way, 2, firsts[way], zr.at[way, 0])
    for way, d in ((0, 3), (1, 5)):
        has_z(d)
        own_z(d, every)
        along(0, d, way, 1, firsts[way], zr.at[way, 1])
    for way, d in ((0, 3), (1, 5)):
        along(0, d, way, 1, seconds[way], zr.at[way, 2])
    for d in (2, 1, 3):
        own_y(d, 4)
    sib_z(1), sib_z(7)
    for way, d in ((0, 1), (1, 7)):
        has_z(d)
        own_z(d, every)
        along(2, d, way, 1, every, last_z)
    sib_z(2), sib_z(6), sib_y(0), sib_z(0)
    for way, d in ((0, 2), (1, 6)):
        has_z(d)
        wait_z(1, way, firsts[way], zr.at[way, 0])
        wait_z(0, way, firsts[way], zr.at[way, 1])
        own_z(d, firsts[way], (way * 4, way * 4 + 1))
        along(3, d, way, 2, firsts[way], last_z)
    for way, d in ((0, 2), (1, 6)):
        wait_z(0, way, seconds[way], zr.at[way, 2])
        own_z(d, seconds[way], (way * 4,))
        along(3, d, way, 2, seconds[way], last_z)

    has_y(0)
    for h in range(2):
        arrived(ry.at[pl.ds(1, 3), pl.ds(4 * h, 4)], yr.at[h])
        for k in range(4 * h, 4 * h + 4):
            d = z_order[k]
            v = sum_y(0, k) + (ry[1, k].astype(F32) + ry[2, k].astype(F32)) + ry[3, k].astype(F32)
            if d:
                o2[d] = v.astype(BF16)
                send(o2.at[d], r2.at[d], s2, q2, off_z(d))
            else:
                keep[...] = v
    has_z(0)
    arrived(rz.at[pl.ds(0, 4)], last_z)
    for k in range(NY):
        v = sum_z(0, k) + (rz[2, k].astype(F32) + rz[3, k].astype(F32)) + (rz[6, k].astype(F32) + rz[7, k].astype(F32))
        r3[y, k] = v.astype(BF16)
    for d in (2, 1, 3):
        send(r3.at[y], r3.at[y], s3, q3, off_y(d))

    def blk(j, zz, yy, n=1):
        return g.at[pl.ds((c * 2 + j) * (UPPER // 4) + ((zz + NZ) % NZ) * NY + (yy + NY) % NY, n)]

    def solve(right, total, factor):
        v = (right - total).astype(BF16)
        h = lax.dot_general(v, factor, NT, preferred_element_type=F32).astype(BF16)
        return lax.dot_general(h, factor, NN, preferred_element_type=F32)

    def out1(d):
        b = blk(1, z - d, y)
        for dy in (2, 1, 3):
            send(b, b, gs, ayr.at[d], off_y(dy))
        send(b, b, gs, br, sibling)

    total = keep[...]
    arrived(r2.at[pl.ds(1, NZ - 1)], q2)
    for d in range(1, NZ):
        total = total + r2[d].astype(F32)
    v = solve(ur1[...], total, ui1[...])
    us[1] = v
    g[(c * 2 + 1) * (UPPER // 4) + z * NY + y] = v.astype(BF16)
    b = blk(1, z, y)
    for d in (4, 3, 5, 2, 6, 1, 7):
        send(b, b, gs, azr.at[d], off_z(d))
    out1(0)

    arrived(ui.at[pl.ds(0, NY - 1)], mr.at[0])
    arrived(ur.at[pl.ds(0, NY - 1)], mr.at[1])
    arrived(r3.at[pl.ds(0, NY - 1)], q3)
    for k in range(NY):
        total = (r3[0, k].astype(F32) + r3[1, k].astype(F32)) + (r3[2, k].astype(F32) + r3[3, k].astype(F32))
        v = solve(ur[k], total, ui[k])
        solved_y[k] = v
        g[c * 2 * (UPPER // 4) + z * NY + k] = v.astype(BF16)
    us[0] = solved_y[y]

    def in1(d):
        arrived(blk(1, z - d, y), azr.at[d])
        out1(d)

    def along_y(d):
        arrived(g.at[pl.ds(0, NY - 1)], ayr.at[d])
        for dy in (1, 3, 2):
            b = blk(1, z - d, y - dy)
            send(b, b, gs, br, sibling)

    def ring_piece(way, k, mine=0):
        s, first = ((1, 0), (2, 1), (2, 0), (3, 1), (3, 0), (4, 1))[k]
        s = s - mine
        zz = z - s if way == 0 else z + s
        return (zz, 0, NY) if k == 0 else (zz, 2 * (1 - first if way == 0 else first), 2)

    def hop(way, n):
        return off_z(n if way == 0 else NZ - n)

    def along_z(k):
        for way in range(2):
            b = blk(0, *ring_piece(way, k))
            arrived(b, arr.at[way, k])
            if k in (1, 2):
                send(b, b, gs, arr.at[way, k + 2], hop(way, 1))
            if k == 1:
                send(b, b, gs, arr.at[way, 5], hop(way, 2))
            send(b, b, gs, br, sibling)

    for k in (1, 2, 0):
        for way in range(2):
            b = blk(0, *ring_piece(way, k, 2 if k else 1))
            send(b, b, gs, arr.at[way, k], hop(way, 2 if k else 1))
    b = blk(0, z, 0, NY)
    send(b, b, gs, br, sibling)
    in1(1), in1(7), in1(2), in1(6), in1(3), in1(5), along_y(0), in1(4)
    along_z(1), along_y(1), along_y(7), along_z(2), along_y(2), along_y(6)
    along_z(0), along_y(3), along_y(5), along_z(3), along_z(5), along_y(4), along_z(4)
    arrived(g.at[pl.ds(0, UPPER // 2)], br)

    def backward(i, _):
        backs = []
        for q in range(16):
            n = i * 16 + q
            parts = []
            for b in range(PER):
                k = n * PER + b
                parts.append(g[idx_s[CAP + k // W, k % W]])
            corr = lax.dot_general(
                jnp.concatenate(parts, axis=1), u[pl.ds(n * PER, PER)].reshape(PER * W, W), NN, preferred_element_type=F32
            )
            backs.append((lf[n] - corr).astype(BF16))
        for q in range(16):
            lo[i * 16 + q] = lax.dot_general(backs[q], inv[i * 2 + q // 8, q % 8], NN, preferred_element_type=F32)
        return 0

    lax.fori_loop(0, 2, backward, 0)
    sent(pk.at[pl.ds(0, 3)], xs)
    sent(az, csz)
    sent(ay, csy)
    sent(oz.at[pl.ds(0, 7)], zs)
    sent(oy.at[pl.ds(0, 3)], ys)
    sent(o2.at[pl.ds(0, NZ - 1)], s2)
    sent(r3.at[pl.ds(0, NY - 1)], s3)
    sent(g.at[pl.ds(0, 123)], gs)
    sent(ui.at[pl.ds(0, NY - 1)], ms.at[0])
    sent(ur.at[pl.ds(0, NY - 1)], ms.at[1])


def on_device(leaf_right, upper_right, leaf_inverse, upper_inverse, update_blocks, block_target, upper_place):
    hbm = pl.BlockSpec(memory_space=pltpu.HBM)
    vmem = pl.BlockSpec(memory_space=pltpu.VMEM)
    dma = pltpu.SemaphoreType.DMA
    leaves = NX * GROUP
    half = lambda *shape: pltpu.VMEM(shape + (COLS, W), BF16)
    wide = lambda *shape: pltpu.VMEM(shape + (COLS, W), F32)
    return pl.pallas_call(
        kernel,
        out_shape=(pltpu.VMEM((leaves, COLS, W), F32), pltpu.VMEM((2, COLS, W), F32)),
        in_specs=[hbm] * 7,
        out_specs=(vmem, vmem),
        scratch_shapes=[
            pltpu.VMEM((1, BLOCKS), I32),
            pltpu.VMEM((1, W), I32),
            pltpu.VMEM((BLOCKS, W, W), BF16),
            wide(leaves),
            pltpu.VMEM((NX, 2, 2, 9, STRIP, W), BF16),
            pltpu.VMEM((NX, GROUP, W, W), BF16),
            wide(leaves),
            wide(BLOCKS + 1),
            pltpu.VMEM((8, W), I32),
            pltpu.SMEM((8, W), I32),
            half(NZ, NY), half(NY, NZ),
            half(NZ, NY), half(NY, NZ),
            half(NZ, NY), half(NY, NZ),
            half(8, NY), half(NY, NZ),
            half(NZ), half(NZ),
            half(NY, NY),
            wide(),
            wide(NY),
            pltpu.VMEM((NY, W, W), BF16),
            wide(),
            pltpu.VMEM((W, W), BF16),
            wide(NY),
            half(UPPER),
            dma((17,)),
            dma((6, 2)),
            dma((NZ,)), dma((NY,)),
            dma((2, 3)), dma, dma((2,)),
            dma, dma,
            dma((NZ,)), dma((NZ,)), dma((2, 6)), dma, dma((2,)),
            dma, dma, dma, dma, dma, dma, dma, dma,
            dma((2,)),
            pltpu.SemaphoreType.REGULAR((3,)),
        ],
        compiler_params=pltpu.CompilerParams(
            collective_id=0, has_side_effects=True, vmem_limit_bytes=59 * 2**20
        ),
        name="solve",
    )(block_target.reshape(1, -1), upper_place.reshape(1, -1), leaf_right, upper_right, leaf_inverse, upper_inverse, update_blocks)


def solution(mesh):
    return jax.shard_map(
        on_device,
        mesh=mesh,
        in_specs=(
            P("leaf", "rhs", None),
            P("leaf", "rhs", None),
            P(("leaf", "rhs"), None, None),
            P("leaf", None, None),
            P("leaf", None, None),
            P("leaf", None),
            P(),
        ),
        out_specs=(P("leaf", "rhs", None), P("leaf", "rhs", None)),
        check_vma=False,
    )
```
